256 devices in a mesh: blk: 128 (over y_lo, z, x, core), grp: 2 (over y_hi).
Axes of the slice: x: 4, y: 4 (y_hi: 2, y_lo: 2; y = y_hi * 2 + y_lo), z: 8, core: 2. Of those that a mesh axis runs over, the one named last changes fastest.
Arguments:
- images: bfloat16 [131072, 1024], P(('blk', 'grp')), may hold values from -6 to 6
- texts: bfloat16 [131072, 1024], P(('blk', 'grp')), may hold values from -6 to 6
- row_lse: bfloat16 [131072], P(('blk', 'grp')), may hold values from 6 to 10
- col_lse: bfloat16 [131072], P(('blk', 'grp')), may hold values from 6 to 10
Outputs:
- grad_image: float32 [131072, 1024], P(('blk', 'grp'))
- grad_text: float32 [131072, 1024], P(('blk', 'grp'))
The draws below stay inside these ranges and needn't reach their ends.
All inputs are finite; a program needn't handle non-finite values.
Results may differ from the reference program's by a relative error of at most 0.0045.
Values may be sent and summed in bfloat16 or wider, within the bound.
A program may use at most 128 MiB of HBM per device.

```python
import math
import jax
import jax.numpy as jnp
from jax import lax

E = 1024
ROWS = 512
STEPS = 2
B = 131072
N_BLK = 128
N_GRP = 2


def shard_levels(rng, extent, split, smallest, high):
    factor_of = 1.0
    for dim, blocks in split:
        steps = jax.random.uniform(jax.random.fold_in(jax.random.fold_in(rng, 6), dim), (blocks,), jnp.float32, smallest / len(split), high / len(split))
        factor_of = factor_of * jnp.repeat(jnp.exp(steps), extent[dim] // blocks).reshape((-1,) + (1,) * (len(extent) - 1 - dim))
    return factor_of


def scatter_about(rng, extent, spread, bound, cuts=(), kind=jnp.bfloat16):
    entries = jax.random.normal(rng, extent, jnp.float32) * spread
    if len(cuts) > 0:
        entries = shard_levels(rng, extent, cuts, -0.22, 0.18) * entries
    return jnp.clip(entries, min=-bound, max=bound).astype(kind)


def setup_inputs(seed: int = 0) -> dict:
    arg_keys = jax.random.split(jax.random.key(seed), 5)
    images = scatter_about(arg_keys[0], (B, E), 1.0, 6.0, ((0, 256),))
    texts = scatter_about(arg_keys[1], (B, E), 1.0, 6.0, ((0, 256),))
    row_lse = jnp.clip(6.0 + 4.0 * jax.random.uniform(arg_keys[2], (B,), jnp.float32) ** shard_levels(arg_keys[2], (B,), ((0, 256),), -0.2, 0.2), 6.0, 10.0).astype(jnp.bfloat16)
    col_lse = jnp.clip(6.0 + 4.0 * jax.random.uniform(arg_keys[3], (B,), jnp.float32) ** shard_levels(arg_keys[3], (B,), ((0, 256),), -0.2, 0.2), 6.0, 10.0).astype(jnp.bfloat16)
    return {"images": images, "texts": texts, "row_lse": row_lse, "col_lse": col_lse}


def reference(images, texts, row_lse, col_lse):
    span = ROWS * N_GRP
    scale = 2.0 / math.sqrt(E)
    imgs = images.reshape(N_BLK, span, E)
    txts = texts.reshape(N_BLK, span, E)
    rows = row_lse.reshape(N_BLK, span).astype(jnp.float32)
    cols = col_lse.reshape(N_BLK, span).astype(jnp.float32)
    grad_img = jnp.zeros((N_BLK, span, E), jnp.float32)
    grad_txt = jnp.zeros((N_BLK, span, E), jnp.float32)
    for step in range(STEPS + 1):
        moved = jnp.roll(txts, step, axis=0)
        moved_cols = jnp.roll(cols, step, axis=0)
        if step == 0:
            diagonal = 2.0 * jnp.eye(span, dtype=jnp.float32)
        else:
            diagonal = jnp.zeros((span, span), jnp.float32)

        def one_block(pieces):
            img, txt, row_part, col_part = pieces
            scores = jnp.dot(img, txt.T, preferred_element_type=jnp.float32) * scale
            weights = jnp.exp(scores - row_part[:, None]) + jnp.exp(scores - col_part[None, :]) - diagonal
            weights = weights.astype(jnp.bfloat16)
            part_img = jnp.dot(weights, txt, preferred_element_type=jnp.float32)
            part_txt = jnp.dot(weights.T, img, preferred_element_type=jnp.float32)
            return (part_img, part_txt)
        part_img, part_txt = lax.map(one_block, (imgs, moved, rows, moved_cols))
        grad_img = grad_img + part_img
        grad_txt = grad_txt + jnp.roll(part_txt, -step, axis=0)
    return (grad_img.reshape(N_BLK * span, E), grad_txt.reshape(N_BLK * span, E))
```

```python
import functools
import math

import jax
import jax.numpy as jnp
from jax import lax
from jax.experimental import pallas as pl
from jax.experimental.pallas import tpu as pltpu
from jax.sharding import PartitionSpec as P

MESH = pl.DeviceIdType.MESH
LSE_TOP = 10.0
LOG2E = math.log2(math.e)


def kernel(
    n_blk,
    scale,
    texts_in,
    images_in,
    factors_in,
    grad_img_out,
    grad_txt_out,
    txt,
    img,
    row_f,
    col_f,
    col_c,
    acc_t,
    acc_i,
    out_t,
    out_1,
    out_2,
    in_t,
    in_1,
    in_2,
    load_sem,
    send_sem,
    recv_sem,
    f_send,
    f_recv,
    store_sem,
):
    rows = texts_in.shape[0]
    half = rows // 2
    c = lax.axis_index("blk")
    h = lax.axis_index("grp")
    core = lax.rem(c, 2)
    other = (c, 1 - h)
    sibling = (c + 1 - 2 * core, h)
    ahead = (lax.rem(c + 2, n_blk), h)
    behind = (lax.rem(c + n_blk - 2, n_blk), h)

    def piece(j):
        return pl.ds(j * half, half)

    def remote(kind, j, src, dst, to):
        return pltpu.make_async_remote_copy(
            src_ref=src,
            dst_ref=dst,
            send_sem=send_sem.at[kind, j],
            recv_sem=recv_sem.at[kind, j],
            device_id=to,
            device_id_type=MESH,
        )

    def remote_f(kind, src, dst, to):
        return pltpu.make_async_remote_copy(
            src_ref=src,
            dst_ref=dst,
            send_sem=f_send.at[kind],
            recv_sem=f_recv.at[kind],
            device_id=to,
            device_id_type=MESH,
        )

    def other_rows(j):
        return pl.ds(rows + j * half, half)

    cp_t = [remote(0, j, txt.at[piece(j)], txt.at[other_rows(j)], other) for j in range(2)]
    cp_2 = [remote(1, j, img.at[0, piece(j)], img.at[2, piece(j)], behind) for j in range(2)]
    cp_1own = [remote(2, j, img.at[0, piece(j)], img.at[1, piece(j)], sibling) for j in range(2)]
    cp_1fwd = [remote(2, j, img.at[2, piece(j)], img.at[1, piece(j)], sibling) for j in range(2)]
    cf_t = remote_f(0, col_f.at[0], col_f.at[1], other)
    cf_2 = remote_f(1, row_f.at[0], row_f.at[2], behind)
    cf_1own = remote_f(2, row_f.at[0], row_f.at[1], sibling)
    cf_1fwd = remote_f(2, row_f.at[2], row_f.at[1], sibling)
    cp_gt = [remote(3, j, out_t.at[piece(j)], in_t.at[piece(j)], other) for j in range(2)]
    cp_g1 = [remote(4, j, out_1.at[piece(j)], in_1.at[piece(j)], sibling) for j in range(2)]
    cp_g2 = [remote(5, j, out_2.at[piece(j)], in_2.at[piece(j)], ahead) for j in range(2)]

    load_t = pltpu.make_async_copy(texts_in, txt.at[pl.ds(0, rows)], load_sem.at[0])
    load_i = pltpu.make_async_copy(images_in, img.at[0], load_sem.at[1])
    load_t.start()
    load_i.start()

    barrier = pltpu.get_barrier_semaphore()
    for device in (other, sibling, ahead, behind):
        pl.semaphore_signal(barrier, inc=1, device_id=device, device_id_type=MESH)

    row_f[0] = factors_in[0:8, :]
    col_f[0] = factors_in[8:16, :]
    load_t.wait()
    load_i.wait()
    pl.semaphore_wait(barrier, 4)

    cf_t.start()
    cf_2.start()
    for j in range(2):
        cp_t[j].start()
        cp_2[j].start()

    @pl.when(core == 1)
    def _():
        cf_1own.start()
        for j in range(2):
            cp_1own[j].start()

    acc_t[...] = jnp.zeros(acc_t.shape, jnp.float32)
    acc_i[...] = jnp.zeros(acc_i.shape, jnp.float32)

    def spread(g):
        wide = jnp.broadcast_to(col_f[g, 0:1, :], (128, rows))
        col_c[pl.ds(g * rows, rows), :] = wide.T

    spread(0)

    def tile(tc, d, lo, n, diagonal=False):
        t_rows = pl.ds(pl.multiple_of(tc * half, half), half)
        t = txt[t_rows, :]
        i = img[d, pl.ds(lo, n), :]
        s = lax.dot_general(t, i, (((1,), (1,)), ((), ())), preferred_element_type=jnp.float32)
        col = jnp.concatenate([col_c[t_rows, :]] * (n // 128), axis=1)
        row = row_f[d, 0:1, pl.ds(lo, n)]
        w = jnp.exp2(s * (scale * LOG2E) - LSE_TOP * LOG2E) * (col + row)
        if diagonal:
            t_id = lax.broadcasted_iota(jnp.int32, (half, n), 0) + tc * half
            i_id = lax.broadcasted_iota(jnp.int32, (half, n), 1) + lo
            w = w - jnp.where(t_id == i_id, 2.0, 0.0)
        w = w.astype(jnp.bfloat16)
        acc_t[t_rows, :] += jnp.dot(w, i, preferred_element_type=jnp.float32)
        acc_i[d, pl.ds(lo, n), :] += lax.dot_general(
            w, t, (((0,), (0,)), ((), ())), preferred_element_type=jnp.float32
        )

    def loop(count, body):
        lax.fori_loop(0, count, lambda k, _: (body(k), 0)[1], 0)

    loop(2, lambda k: tile(k, 0, 0, rows, True))

    def arrive(j):
        cp_2[j].wait_recv()

        @pl.when(core == 0)
        def _():
            cp_1fwd[j].start()

        cp_1own[j].wait_recv()

    cf_2.wait_recv()

    @pl.when(core == 0)
    def _():
        cf_1fwd.start()

    cf_1own.wait_recv()
    arrive(0)
    loop(4, lambda k: tile(lax.rem(k, 2), 1 + k // 2, 0, half))
    cf_t.wait_recv()
    spread(1)
    cp_t[0].wait_recv()
    tile(2, 0, 0, rows)
    loop(2, lambda k: tile(2, 1 + k, 0, half))
    arrive(1)
    loop(2, lambda k: tile(2, 1 + k, half, half))
    out_t[piece(0), :] = acc_t[pl.ds(rows, half), :].astype(jnp.bfloat16)
    cp_gt[0].start()
    loop(4, lambda k: tile(lax.rem(k, 2), 1 + k // 2, half, half))
    cp_t[1].wait_recv()
    loop(3, lambda k: tile(3, k, 0, rows))
    out_1[...] = acc_i[1].astype(jnp.bfloat16)
    for j in range(2):
        cp_g1[j].start()
    out_t[piece(1), :] = acc_t[pl.ds(rows + half, half), :].astype(jnp.bfloat16)
    cp_gt[1].start()

    @pl.when(core == 0)
    def _():
        for j in range(2):
            cp_g1[j].wait_recv()
            out_2[piece(j), :] = (acc_i[2, piece(j), :] + in_1[piece(j), :].astype(jnp.float32)).astype(jnp.bfloat16)
            cp_g2[j].start()

    @pl.when(core == 1)
    def _():
        for j in range(2):
            out_2[piece(j), :] = acc_i[2, piece(j), :].astype(jnp.bfloat16)
            cp_g2[j].start()
        for j in range(2):
            cp_g1[j].wait_recv()
            acc_i[0, piece(j), :] += in_1[piece(j), :].astype(jnp.float32)

    stores = []
    for j in range(2):
        cp_gt[j].wait_recv()
        acc_t[piece(j), :] += in_t[piece(j), :].astype(jnp.float32)
        stores.append(pltpu.make_async_copy(acc_t.at[piece(j)], grad_txt_out.at[piece(j)], store_sem.at[0, j]))
        stores[-1].start()
        cp_g2[j].wait_recv()
        acc_i[0, piece(j), :] += in_2[piece(j), :].astype(jnp.float32)
        stores.append(pltpu.make_async_copy(acc_i.at[0, piece(j)], grad_img_out.at[piece(j)], store_sem.at[1, j]))
        stores[-1].start()
    for store in stores:
        store.wait()

    cf_t.wait_send()
    cf_2.wait_send()
    cf_1own.wait_send()
    for j in range(2):
        cp_t[j].wait_send()
        cp_2[j].wait_send()
        cp_1own[j].wait_send()
        cp_gt[j].wait_send()
        cp_g1[j].wait_send()
        cp_g2[j].wait_send()


def local(n_blk, images, texts, row_lse, col_lse):
    rows, width = images.shape
    scale = 2.0 / math.sqrt(width)
    lse = jnp.stack([row_lse, col_lse]).astype(jnp.float32)
    factors = jnp.exp(LSE_TOP - jnp.repeat(lse, 8, axis=0))
    bf16, f32 = jnp.bfloat16, jnp.float32
    grad_img, grad_txt = pl.pallas_call(
        functools.partial(kernel, n_blk, scale),
        out_shape=[jax.ShapeDtypeStruct((rows, width), f32)] * 2,
        in_specs=[
            pl.BlockSpec(memory_space=pl.ANY),
            pl.BlockSpec(memory_space=pl.ANY),
            pl.BlockSpec(memory_space=pltpu.VMEM),
        ],
        out_specs=[pl.BlockSpec(memory_space=pl.ANY)] * 2,
        scratch_shapes=[
            pltpu.VMEM((2 * rows, width), bf16),
            pltpu.VMEM((3, rows, width), bf16),
            pltpu.VMEM((3, 8, rows), f32),
            pltpu.VMEM((2, 8, rows), f32),
            pltpu.VMEM((2 * rows, 128), f32),
            pltpu.VMEM((2 * rows, width), f32),
            pltpu.VMEM((3, rows, width), f32),
        ]
        + [pltpu.VMEM((rows, width), bf16)] * 6
        + [
            pltpu.SemaphoreType.DMA((2,)),
            pltpu.SemaphoreType.DMA((6, 2)),
            pltpu.SemaphoreType.DMA((6, 2)),
            pltpu.SemaphoreType.DMA((3,)),
            pltpu.SemaphoreType.DMA((3,)),
            pltpu.SemaphoreType.DMA((2, 2)),
        ],
        compiler_params=pltpu.CompilerParams(
            collective_id=0, has_side_effects=True, vmem_limit_bytes=48 * 2**20
        ),
        cost_estimate=pl.CostEstimate(
            flops=18 * 2 * rows * rows * width,
            bytes_accessed=12 * rows * width,
            transcendentals=6 * rows * rows,
        ),
        name="contrastive",
    )(texts, images, factors)
    return (grad_img, grad_txt)


def solution(mesh):
    both = ("blk", "grp")
    return jax.shard_map(
        functools.partial(local, mesh.shape["blk"]),
        mesh=mesh,
        in_specs=(P(both, None), P(both, None), P(both), P(both)),
        out_specs=(P(both, None), P(both, None)),
        check_vma=False,
    )
```

```python
import functools
import math

import jax
import jax.numpy as jnp
from jax import lax
from jax.experimental import pallas as pl
from jax.experimental.pallas import tpu as pltpu
from jax.sharding import PartitionSpec as P

MESH = pl.DeviceIdType.MESH
LSE_TOP = 10.0
LOG2E = math.log2(math.e)
PIECES = 4
NX, NZ = 4, 8
ROUTES = (
    (3, 7, 0, 64),
    (1, 1, 64, 64),
    (0, 7, 128, 64),
    (2, 1, 192, 64),
    (1, 2, 256, 64),
    (2, 2, 320, 64),
    (1, 0, 384, 32),
    (2, 0, 416, 32),
    (1, 7, 448, 32),
    (2, 7, 480, 32),
)


def kernel(
    n_blk,
    scale,
    texts_in,
    images_in,
    factors_in,
    grad_img,
    grad_txt,
    txt,
    img,
    row_f,
    col_f,
    row_c,
    col_c,
    acc_t,
    acc_i,
    out_t,
    out_1,
    out_2,
    in_t,
    in_1,
    in_2,
    load_sem,
    send_sem,
    recv_sem,
    f_send,
    f_recv,
    go_sem,
    relay,
    relay_send,
    relay_recv,
):
    rows = texts_in.shape[0]
    half = rows // 2
    part = rows // PIECES
    c = lax.axis_index("blk")
    h = lax.axis_index("grp")
    core = lax.rem(c, 2)
    other = (c, 1 - h)
    sibling = (c + 1 - 2 * core, h)
    ahead = (lax.rem(c + 2, n_blk), h)
    behind = (lax.rem(c + n_blk - 2, n_blk), h)

    x, z, y = lax.rem(c // 2, NX), lax.rem(c // (2 * NX), NZ), c // (2 * NX * NZ)

    def chip(cx, cz, cy):
        return ((cy * NZ + cz) * NX + cx) * 2 + core, h

    def is_at(cx, cz):
        return jnp.logical_and(x == cx, z == cz)

    first, last = is_at(0, 0), is_at(NX - 1, NZ - 1)
    to_last = [(cx, cz, r, n) for cx, cz, r, n in ROUTES]
    to_first = [(NX - 1 - cx, NZ - 1 - cz, r, n) for cx, cz, r, n in ROUTES]

    def piece(j, base=0):
        return pl.ds(pl.multiple_of(base + j * part, part), part)

    def remote(src, dst, sends, recvs, to):
        return pltpu.make_async_remote_copy(
            src_ref=src, dst_ref=dst, send_sem=sends, recv_sem=recvs, device_id=to, device_id_type=MESH
        )

    def remote_k(kind, j, src, dst, to):
        return remote(src, dst, send_sem.at[kind, j], recv_sem.at[kind, j], to)

    def send_t(j):
        return remote_k(0, j, texts_in.at[piece(j)], txt.at[piece(j, rows)], other)

    def send_2(j):
        return remote_k(1, j, images_in.at[piece(j)], img.at[2, piece(j)], behind)

    def send_1(j):
        return remote_k(2, j, images_in.at[piece(j)], img.at[1, piece(j)], sibling)

    def pass_1(j):
        return remote_k(2, j, img.at[2, piece(j)], img.at[1, piece(j)], sibling)

    def back_t(j):
        return remote_k(3, j, out_t.at[piece(j)], in_t.at[piece(j)], other)

    def back_1(j):
        return remote_k(4, j, out_1.at[piece(j)], in_1.at[piece(j)], sibling)

    def back_2(j):
        return remote_k(5, j, out_2.at[piece(j)], in_2.at[piece(j)], ahead)

    def launch(plain, routes, source, final, src, dst, kind, slot, j):
        @pl.when(jnp.logical_not(is_at(*source)))
        def _():
            plain(j).start()

        @pl.when(is_at(*source))
        def _():
            for cx, cz, r, n in routes:
                if r // part != j:
                    continue
                sem = send_sem.at[kind, j]
                if (cx, cz) == final:
                    copy = remote(src.at[pl.ds(r, n)], dst.at[pl.ds(r, n)], sem, recv_sem.at[kind, j], chip(cx, cz, 1 - y))
                else:
                    there = relay.at[slot, pl.ds(0, n)]
                    copy = remote(src.at[pl.ds(r, n)], there, sem, relay_recv.at[slot], chip(cx, cz, 1 - y))
                copy.start()

    FIRST, LAST = (0, 0), (NX - 1, NZ - 1)

    def start_2(j):
        launch(send_2, to_last, FIRST, LAST, images_in, img.at[2], 1, 0, j)

    def start_back(j):
        launch(back_2, to_first, LAST, FIRST, out_2, in_2, 5, 1, j)

    def on_route(routes, final, slot, kind, dst, done):
        for cx, cz, r, n in routes:
            if (cx, cz) == final:
                continue

            @pl.when(is_at(cx, cz))
            def _():
                here = relay.at[slot, pl.ds(0, n)]
                if not done:
                    remote(here, here, relay_send.at[slot], relay_recv.at[slot], chip(*final, y)).wait_recv()
                copy = remote(here, dst.at[pl.ds(r, n)], relay_send.at[slot], recv_sem.at[kind, r // part], chip(*final, y))
                if done:
                    copy.wait_send()
                else:
                    copy.start()

    def pass_2(done=False):
        on_route(to_last, LAST, 0, 1, img.at[2], done)

    def pass_back(done=False):
        on_route(to_first, FIRST, 1, 5, in_2, done)

    f_t = remote(col_f.at[0], col_f.at[1], f_send.at[0], f_recv.at[0], other)
    f_2 = remote(row_f.at[0], row_f.at[2], f_send.at[1], f_recv.at[1], behind)
    f_1 = remote(row_f.at[0], row_f.at[1], f_send.at[2], f_recv.at[2], sibling)
    f_1_pass = remote(row_f.at[2], row_f.at[1], f_send.at[2], f_recv.at[2], sibling)

    load_t = pltpu.make_async_copy(texts_in, txt.at[pl.ds(0, rows)], load_sem.at[0])
    load_i = pltpu.make_async_copy(images_in, img.at[0], load_sem.at[1])

    barrier = pltpu.get_barrier_semaphore()
    for device in (other, sibling, ahead, behind):
        pl.semaphore_signal(barrier, inc=1, device_id=device, device_id_type=MESH)

    def greet(device):
        pl.semaphore_signal(barrier, inc=1, device_id=device, device_id_type=MESH)

    greetings = 4
    for routes, source, final in ((to_last, FIRST, LAST), (to_first, LAST, FIRST)):
        between = [(cx, cz) for cx, cz, r, n in routes if (cx, cz) != final]
        greetings += jnp.where(is_at(*source), len(between), 0)
        for cx, cz in between:
            greetings += jnp.where(is_at(cx, cz), 1, 0)

            @pl.when(is_at(cx, cz))
            def _():
                greet(chip(*source, 1 - y))

        @pl.when(is_at(*final))
        def _():
            for cx, cz in between:
                greet(chip(cx, cz, y))

    load_t.start()
    load_i.start()
    row_f[0] = factors_in[0:8, :]
    col_f[0] = factors_in[8:16, :]
    pl.semaphore_wait(barrier, greetings)

    f_t.start()
    f_2.start()

    @pl.when(core == 0)
    def _():
        for j in range(PIECES):
            start_2(j)

    @pl.when(core == 1)
    def _():
        f_1.start()
        for j in range(PIECES):
            send_t(j).start()
        for j in range(PIECES):
            send_1(j).start()

    acc_t[...] = jnp.zeros(acc_t.shape, jnp.float32)
    acc_i[...] = jnp.zeros(acc_i.shape, jnp.float32)

    def upright(line):
        return jnp.broadcast_to(line, (128, rows)).T

    col_c[pl.ds(0, rows), :] = upright(col_f[0, 0:1, :])

    def weights(s, upright_f, line_f):
        wide = jnp.concatenate([upright_f] * (s.shape[1] // 128), axis=1)
        return jnp.exp2(s * (scale * LOG2E) - LSE_TOP * LOG2E) * (wide + line_f)

    def scores(a, b):
        return lax.dot_general(a, b, (((1,), (1,)), ((), ())), preferred_element_type=jnp.float32)

    def times(a, b):
        return jnp.dot(a, b, preferred_element_type=jnp.float32)

    def turned_times(a, b):
        return lax.dot_general(a, b, (((0,), (0,)), ((), ())), preferred_element_type=jnp.float32)

    def text_half(k, d, diagonal=False):
        at = pl.ds(pl.multiple_of(k * half, half), half)
        t, i = txt[at, :], img[d]
        w = weights(scores(t, i), col_c[at, :], row_f[d, 0:1, :])
        if diagonal:
            t_id = lax.broadcasted_iota(jnp.int32, w.shape, 0) + k * half
            i_id = lax.broadcasted_iota(jnp.int32, w.shape, 1)
            w = w - jnp.where(t_id == i_id, 2.0, 0.0)
        w = w.astype(jnp.bfloat16)
        acc_t[at, :] += times(w, i)
        acc_i[d] += turned_times(w, t)

    def image_half(d, k, g):
        at = pl.ds(pl.multiple_of(k * half, half), half)
        t_at = pl.ds(pl.multiple_of(g * rows, rows), rows)
        t, i = txt[t_at, :], img[d, at, :]
        w = weights(scores(i, t), row_c[d, at, :], col_f[g, 0:1, :]).astype(jnp.bfloat16)
        acc_i[d, at, :] += times(w, t)
        acc_t[t_at, :] += turned_times(w, i)

    def loop(count, body):
        def step(k, carry):
            body(k)
            return carry

        lax.fori_loop(0, count, step, 0)

    load_t.wait()
    load_i.wait()
    loop(2, lambda k: text_half(k, 0, True))

    @pl.when(core == 0)
    def _():
        def take(j):
            send_2(j).wait_recv()
            pass_1(j).start()

        f_2.wait_recv()
        f_1_pass.start()
        row_c[2] = upright(row_f[2, 0:1, :])
        take(0)
        f_1.wait_recv()
        for j in range(PIECES):
            send_1(j).wait_recv()
        loop(2, lambda k: text_half(k, 1))

        def both(k):
            @pl.when(k == 0)
            def _():
                take(1)
                pass_2()

            @pl.when(k == 1)
            def _():
                pl.semaphore_wait(go_sem, 1)
                for j in range(PIECES):
                    send_t(j).start()
                take(2)
                take(3)

            image_half(2, k, 0)

        loop(2, both)
        f_t.wait_recv()
        col_c[pl.ds(rows, rows), :] = upright(col_f[1, 0:1, :])
        send_t(0).wait_recv()
        send_t(1).wait_recv()
        loop(3, lambda d: text_half(2, d))
        out_t[pl.ds(0, half), :] = acc_t[pl.ds(rows, half), :].astype(jnp.bfloat16)
        send_t(2).wait_recv()
        send_t(3).wait_recv()
        back_t(0).start()
        back_t(1).start()

        def ending(k):
            text_half(3, 2 - k)

            @pl.when(k == 0)
            def _():
                def on(j):
                    back_1(j).wait_recv()
                    both = acc_i[2, piece(j), :] + in_1[piece(j), :].astype(jnp.float32)
                    out_2[piece(j), :] = both.astype(jnp.bfloat16)
                    start_back(j)

                for j in range(PIECES):
                    on(j)

            @pl.when(k == 1)
            def _():
                out_1[...] = acc_i[1].astype(jnp.bfloat16)
                loop(PIECES, lambda j: back_1(j).start())

        loop(3, ending)
        out_t[pl.ds(half, half), :] = acc_t[pl.ds(rows + half, half), :].astype(jnp.bfloat16)
        back_t(2).start()
        back_t(3).start()

    @pl.when(core == 1)
    def _():
        f_t.wait_recv()
        col_c[pl.ds(rows, rows), :] = upright(col_f[1, 0:1, :])
        send_t(0).wait_recv()
        send_t(1).wait_recv()
        text_half(2, 0)
        send_t(2).wait_recv()
        pl.semaphore_signal(go_sem, inc=1, device_id=sibling, device_id_type=MESH)
        f_1.wait_recv()
        row_c[1] = upright(row_f[1, 0:1, :])

        def near(k):
            send_1(2 * k).wait_recv()

            @pl.when(k == 1)
            def _():
                for j in range(PIECES):
                    start_2(j)

            send_1(2 * k + 1).wait_recv()
            image_half(1, k, 0)

        loop(2, near)
        pass_2()
        send_t(3).wait_recv()

        def beside(k):
            text_half(2 + jnp.minimum(k, 1), 1 - k // 2)

            @pl.when(k == 1)
            def _():
                out_1[...] = acc_i[1].astype(jnp.bfloat16)
                loop(PIECES, lambda j: back_1(j).start())

        loop(3, beside)
        f_2.wait_recv()
        row_c[2] = upright(row_f[2, 0:1, :])

        def far(k):
            send_2(2 * k).wait_recv()
            send_2(2 * k + 1).wait_recv()

            def side(g):
                image_half(2, k, 1 - g)

                @pl.when(jnp.logical_and(k == 1, g == 0))
                def _():
                    out_t[...] = acc_t[pl.ds(rows, rows), :].astype(jnp.bfloat16)
                    loop(PIECES, lambda j: back_t(j).start())

            loop(2, side)
            at = pl.ds(pl.multiple_of(k * half, half), half)
            out_2[at, :] = acc_i[2, at, :].astype(jnp.bfloat16)
            for j in range(2):

                @pl.when(k == j)
                def _():
                    start_back(2 * j)
                    start_back(2 * j + 1)

        loop(2, far)

        def near_back(j):
            back_1(j).wait_recv()
            acc_i[0, piece(j), :] += in_1[piece(j), :].astype(jnp.float32)

        loop(PIECES, near_back)

    pass_back()

    def finish(j):
        back_t(j).wait_recv()
        grad_txt[piece(j), :] = acc_t[piece(j), :] + in_t[piece(j), :].astype(jnp.float32)
        back_2(j).wait_recv()
        grad_img[piece(j), :] = acc_i[0, piece(j), :] + in_2[piece(j), :].astype(jnp.float32)

    loop(PIECES, finish)

    f_t.wait_send()
    f_2.wait_send()
    f_1.wait_send()

    def sent(j):
        for copy in (send_t, send_2, send_1, back_t, back_1, back_2):
            copy(j).wait_send()

    loop(PIECES, sent)

    pass_2(done=True)
    pass_back(done=True)


def store(grad_img, grad_txt, img_out, txt_out, sem):
    copies = [
        pltpu.make_async_copy(grad_img, img_out, sem.at[0]),
        pltpu.make_async_copy(grad_txt, txt_out, sem.at[1]),
    ]
    for copy in copies:
        copy.start()
    for copy in copies:
        copy.wait()


def local(n_blk, images, texts, row_lse, col_lse):
    rows, width = images.shape
    scale = 2.0 / math.sqrt(width)
    lse = jnp.stack([row_lse, col_lse]).astype(jnp.float32)
    factors = jnp.exp(LSE_TOP - jnp.repeat(lse, 8, axis=0))
    bf16, f32 = jnp.bfloat16, jnp.float32
    any_spec = pl.BlockSpec(memory_space=pl.ANY)
    hbm_spec = pl.BlockSpec(memory_space=pltpu.HBM)
    vmem_spec = pl.BlockSpec(memory_space=pltpu.VMEM)
    grads = pl.pallas_call(
        functools.partial(kernel, n_blk, scale),
        out_shape=[pltpu.VMEM((rows, width), f32)] * 2,
        in_specs=[hbm_spec, hbm_spec, vmem_spec],
        out_specs=[vmem_spec] * 2,
        scratch_shapes=[
            pltpu.VMEM((2 * rows, width), bf16),
            pltpu.VMEM((3, rows, width), bf16),
            pltpu.VMEM((3, 8, rows), f32),
            pltpu.VMEM((2, 8, rows), f32),
            pltpu.VMEM((3, rows, 128), f32),
            pltpu.VMEM((2 * rows, 128), f32),
            pltpu.VMEM((2 * rows, width), f32),
            pltpu.VMEM((3, rows, width), f32),
        ]
        + [pltpu.VMEM((rows, width), bf16)] * 6
        + [
            pltpu.SemaphoreType.DMA((2,)),
            pltpu.SemaphoreType.DMA((6, PIECES)),
            pltpu.SemaphoreType.DMA((6, PIECES)),
            pltpu.SemaphoreType.DMA((3,)),
            pltpu.SemaphoreType.DMA((3,)),
            pltpu.SemaphoreType.REGULAR,
            pltpu.VMEM((2, max(n for _, _, _, n in ROUTES), width), bf16),
            pltpu.SemaphoreType.DMA((2,)),
            pltpu.SemaphoreType.DMA((2,)),
        ],
        compiler_params=pltpu.CompilerParams(
            collective_id=0, has_side_effects=True, vmem_limit_bytes=48 * 2**20
        ),
        cost_estimate=pl.CostEstimate(
            flops=18 * 2 * rows * rows * width,
            bytes_accessed=12 * rows * width,
            transcendentals=6 * rows * rows,
        ),
        name="contrastive",
    )(
        pltpu.with_memory_space_constraint(texts, pltpu.HBM),
        pltpu.with_memory_space_constraint(images, pltpu.HBM),
        factors,
    )
    return tuple(
        pl.pallas_call(
            store,
            out_shape=[jax.ShapeDtypeStruct((rows, width), f32)] * 2,
            in_specs=[vmem_spec] * 2,
            out_specs=[any_spec] * 2,
            scratch_shapes=[pltpu.SemaphoreType.DMA((2,))],
            compiler_params=pltpu.CompilerParams(vmem_limit_bytes=16 * 2**20),
            name="store",
        )(*grads)
    )


def solution(mesh):
    both = ("blk", "grp")
    return jax.shard_map(
        functools.partial(local, mesh.shape["blk"]),
        mesh=mesh,
        in_specs=(P(both, None), P(both, None), P(both), P(both)),
        out_specs=(P(both, None), P(both, None)),
        check_vma=False,
    )
```

```python
import functools
import math

import jax
import jax.numpy as jnp
from jax import lax
from jax.experimental import pallas as pl
from jax.experimental.pallas import tpu as pltpu
from jax.sharding import PartitionSpec as P

MESH = pl.DeviceIdType.MESH
LSE_TOP = 10.0
LOG2E = math.log2(math.e)
PIECES = 4
NX, NZ = 4, 8
ROUTES = (
    (2, 0, 0, 64),
    (2, 1, 64, 64),
    (2, 2, 128, 64),
    (1, 1, 192, 64),
    (2, 3, 256, 64),
    (2, 4, 320, 64),
    (3, 7, 384, 64),
    (0, 7, 448, 64),
)
LATE = ((3, 7), (0, 7))
LATE_PIECE = 3


def kernel(
    n_blk,
    scale,
    texts_in,
    images_in,
    factors_in,
    grad_img,
    grad_txt,
    txt,
    img,
    row_f,
    col_f,
    row_c,
    col_c,
    acc_t,
    acc_i,
    out_t,
    out_1,
    out_2,
    in_t,
    in_1,
    in_2,
    load_sem,
    send_sem,
    recv_sem,
    f_send,
    f_recv,
    go_sem,
    ready_sem,
    relay,
    relay_send,
    relay_recv,
):
    rows = texts_in.shape[0]
    half = rows // 2
    part = rows // PIECES
    c = lax.axis_index("blk")
    h = lax.axis_index("grp")
    core = lax.rem(c, 2)
    other = (c, 1 - h)
    sibling = (c + 1 - 2 * core, h)
    ahead = (lax.rem(c + 2, n_blk), h)
    behind = (lax.rem(c + n_blk - 2, n_blk), h)

    x, z, y = lax.rem(c // 2, NX), lax.rem(c // (2 * NX), NZ), c // (2 * NX * NZ)

    def chip(cx, cz, cy):
        return ((cy * NZ + cz) * NX + cx) * 2 + core, h

    def is_at(cx, cz):
        return jnp.logical_and(x == cx, z == cz)

    first, last = is_at(0, 0), is_at(NX - 1, NZ - 1)
    to_last = [(cx, cz, r, n) for cx, cz, r, n in ROUTES]
    to_first = [(NX - 1 - cx, NZ - 1 - cz, r, n) for cx, cz, r, n in ROUTES]

    def piece(j, base=0):
        return pl.ds(pl.multiple_of(base + j * part, part), part)

    def remote(src, dst, sends, recvs, to):
        return pltpu.make_async_remote_copy(
            src_ref=src, dst_ref=dst, send_sem=sends, recv_sem=recvs, device_id=to, device_id_type=MESH
        )

    def remote_k(kind, j, src, dst, to):
        return remote(src, dst, send_sem.at[kind, j], recv_sem.at[kind, j], to)

    def send_t(j):
        return remote_k(0, j, texts_in.at[piece(j)], txt.at[piece(j, rows)], other)

    def send_2(j):
        return remote_k(1, j, images_in.at[piece(j)], img.at[2, piece(j)], behind)

    def send_1(j):
        return remote_k(2, j, images_in.at[piece(j)], img.at[1, piece(j)], sibling)

    def pass_1(j):
        return remote_k(2, j, img.at[2, piece(j)], img.at[1, piece(j)], sibling)

    def back_t(j):
        return remote_k(3, j, out_t.at[piece(j)], in_t.at[piece(j)], other)

    def back_1(j):
        return remote_k(4, j, out_1.at[piece(j)], in_1.at[piece(j)], sibling)

    def back_2(j):
        return remote_k(5, j, out_2.at[piece(j)], in_2.at[piece(j)], ahead)

    def launch(plain, routes, source, final, src, dst, kind, slot, j):
        @pl.when(jnp.logical_not(is_at(*source)))
        def _():
            plain(j).start()

        @pl.when(is_at(*source))
        def _():
            for cx, cz, r, n in routes:
                if r // part != j:
                    continue
                sem = send_sem.at[kind, j]
                if (cx, cz) == final:
                    copy = remote(src.at[pl.ds(r, n)], dst.at[pl.ds(r, n)], sem, recv_sem.at[kind, j], chip(cx, cz, 1 - y))
                else:
                    there = relay.at[slot, pl.ds(0, n)]
                    copy = remote(src.at[pl.ds(r, n)], there, sem, relay_recv.at[slot], chip(cx, cz, 1 - y))
                copy.start()

    FIRST, LAST = (0, 0), (NX - 1, NZ - 1)

    def start_2(j):
        launch(send_2, to_last, FIRST, LAST, images_in, img.at[2], 1, 0, j)

    def start_back(j):
        launch(back_2, to_first, LAST, FIRST, out_2, in_2, 5, 1, j)

    def on_route(routes, final, slot, kind, dst, done):
        for cx, cz, r, n in routes:
            if (cx, cz) == final:
                continue

            @pl.when(is_at(cx, cz))
            def _():
                here = relay.at[slot, pl.ds(0, n)]
                if not done:
                    if slot == 0 and (cx, cz) not in LATE:
                        pl.semaphore_wait(ready_sem, 1)
                    remote(here, here, relay_send.at[slot], relay_recv.at[slot], chip(*final, y)).wait_recv()
                copy = remote(here, dst.at[pl.ds(r, n)], relay_send.at[slot], recv_sem.at[kind, r // part], chip(*final, y))
                if done:
                    copy.wait_send()
                else:
                    copy.start()

    def pass_2(done=False):
        on_route(to_last, LAST, 0, 1, img.at[2], done)

    def pass_back(done=False):
        on_route(to_first, FIRST, 1, 5, in_2, done)

    f_t = remote(col_f.at[0], col_f.at[1], f_send.at[0], f_recv.at[0], other)
    f_2 = remote(row_f.at[0], row_f.at[2], f_send.at[1], f_recv.at[1], behind)
    f_1 = remote(row_f.at[0], row_f.at[1], f_send.at[2], f_recv.at[2], sibling)
    f_1_pass = remote(row_f.at[2], row_f.at[1], f_send.at[2], f_recv.at[2], sibling)

    load_t = pltpu.make_async_copy(texts_in, txt.at[pl.ds(0, rows)], load_sem.at[0])
    load_i = pltpu.make_async_copy(images_in, img.at[0], load_sem.at[1])

    barrier = pltpu.get_barrier_semaphore()

    def greet(device):
        pl.semaphore_signal(barrier, inc=1, device_id=device, device_id_type=MESH)

    def tell(device):
        pl.semaphore_signal(ready_sem, inc=1, device_id=device, device_id_type=MESH)

    early = [(cx, cz) for cx, cz, _, _ in to_last if (cx, cz) not in LATE]
    late = [(cx, cz) for cx, cz in LATE if (cx, cz) != LAST]
    back = [(cx, cz) for cx, cz, _, _ in to_first if (cx, cz) != FIRST]

    for device in (other, sibling, behind):
        greet(device)

    @pl.when(jnp.logical_not(last))
    def _():
        greet(ahead)

    greetings = 4 + jnp.where(first, len(early) - 1, 0) + jnp.where(last, len(early) + len(back), 0)
    for at in early:

        @pl.when(is_at(*at))
        def _():
            greet(chip(*FIRST, 1 - y))
            greet(chip(*LAST, y))

    for at in late:
        greetings += jnp.where(is_at(*at), 2, 0)
    for at in back:
        greetings += jnp.where(is_at(*at), 1, 0)

        @pl.when(is_at(*at))
        def _():
            greet(chip(*LAST, 1 - y))

    @pl.when(first)
    def _():
        for at in late:
            greet(chip(*at, 1 - y))
        for at in back:
            greet(chip(*at, y))

    @pl.when(last)
    def _():
        for at in late:
            greet(chip(*at, y))

    load_t.start()
    load_i.start()
    row_f[0] = factors_in[0:8, :]
    col_f[0] = factors_in[8:16, :]
    pl.semaphore_wait(barrier, greetings)

    @pl.when(last)
    def _():
        tell(chip(*FIRST, 1 - y))
        for at in early:
            tell(chip(*at, y))

    for at in late:

        @pl.when(is_at(*at))
        def _():
            tell(chip(*FIRST, 1 - y))

    f_t.start()

    @pl.when(jnp.logical_not(first))
    def _():
        f_2.start()


    @pl.when(core == 0)
    def _():
        for j in range(PIECES):
            if j == LATE_PIECE:

                @pl.when(jnp.logical_not(first))
                def _():
                    start_2(j)

            else:
                start_2(j)

    @pl.when(core == 1)
    def _():
        f_1.start()
        for j in range(PIECES):
            send_t(j).start()
        for j in range(PIECES):
            send_1(j).start()

    acc_t[...] = jnp.zeros(acc_t.shape, jnp.float32)
    acc_i[...] = jnp.zeros(acc_i.shape, jnp.float32)

    def upright(line):
        return jnp.broadcast_to(line, (128, rows)).T

    col_c[pl.ds(0, rows), :] = upright(col_f[0, 0:1, :])

    def weights(s, upright_f, line_f):
        wide = jnp.concatenate([upright_f] * (s.shape[1] // 128), axis=1)
        return jnp.exp2(s * (scale * LOG2E) - LSE_TOP * LOG2E) * (wide + line_f)

    def scores(a, b):
        return lax.dot_general(a, b, (((1,), (1,)), ((), ())), preferred_element_type=jnp.float32)

    def times(a, b):
        return jnp.dot(a, b, preferred_element_type=jnp.float32)

    def turned_times(a, b):
        return lax.dot_general(a, b, (((0,), (0,)), ((), ())), preferred_element_type=jnp.float32)

    def text_half(k, d, diagonal=False):
        at = pl.ds(pl.multiple_of(k * half, half), half)
        t, i = txt[at, :], img[d]
        w = weights(scores(t, i), col_c[at, :], row_f[d, 0:1, :])
        if diagonal:
            t_id = lax.broadcasted_iota(jnp.int32, w.shape, 0) + k * half
            i_id = lax.broadcasted_iota(jnp.int32, w.shape, 1)
            w = w - jnp.where(t_id == i_id, 2.0, 0.0)
        w = w.astype(jnp.bfloat16)
        acc_t[at, :] += times(w, i)
        acc_i[d] += turned_times(w, t)

    def image_half(d, k, g):
        at = pl.ds(pl.multiple_of(k * half, half), half)
        t_at = pl.ds(pl.multiple_of(g * rows, rows), rows)
        t, i = txt[t_at, :], img[d, at, :]
        w = weights(scores(i, t), row_c[d, at, :], col_f[g, 0:1, :]).astype(jnp.bfloat16)
        acc_i[d, at, :] += times(w, t)
        acc_t[t_at, :] += turned_times(w, i)

    def loop(count, body):
        def step(k, carry):
            body(k)
            return carry

        lax.fori_loop(0, count, step, 0)

    load_t.wait()
    load_i.wait()
    loop(2, lambda k: text_half(k, 0, True))

    @pl.when(core == 0)
    def _():
        def take(j):
            send_2(j).wait_recv()
            pass_1(j).start()

        f_1.wait_recv()
        for j in range(PIECES):
            send_1(j).wait_recv()
        loop(2, lambda k: text_half(k, 1))

        @pl.when(first)
        def _():
            pl.semaphore_wait(ready_sem, 2)
            f_2.start()
            start_2(LATE_PIECE)

        f_2.wait_recv()
        f_1_pass.start()
        row_c[2] = upright(row_f[2, 0:1, :])
        take(0)

        def both(k):
            @pl.when(k == 0)
            def _():
                take(1)
                pass_2()

            @pl.when(k == 1)
            def _():
                pl.semaphore_wait(go_sem, 1)
                for j in range(PIECES):
                    send_t(j).start()
                take(2)
                take(3)

            image_half(2, k, 0)

        loop(2, both)
        f_t.wait_recv()
        col_c[pl.ds(rows, rows), :] = upright(col_f[1, 0:1, :])
        send_t(0).wait_recv()
        send_t(1).wait_recv()
        loop(3, lambda d: text_half(2, d))
        out_t[pl.ds(0, half), :] = acc_t[pl.ds(rows, half), :].astype(jnp.bfloat16)
        send_t(2).wait_recv()
        send_t(3).wait_recv()
        back_t(0).start()
        back_t(1).start()

        def ending(k):
            text_half(3, 2 - k)

            @pl.when(k == 0)
            def _():
                def on(j):
                    back_1(j).wait_recv()
                    both = acc_i[2, piece(j), :] + in_1[piece(j), :].astype(jnp.float32)
                    out_2[piece(j), :] = both.astype(jnp.bfloat16)
                    start_back(j)

                for j in range(PIECES):
                    on(j)

            @pl.when(k == 1)
            def _():
                out_1[...] = acc_i[1].astype(jnp.bfloat16)
                loop(PIECES, lambda j: back_1(j).start())

        loop(3, ending)
        out_t[pl.ds(half, half), :] = acc_t[pl.ds(rows + half, half), :].astype(jnp.bfloat16)
        back_t(2).start()
        back_t(3).start()

    @pl.when(core == 1)
    def _():
        f_t.wait_recv()
        col_c[pl.ds(rows, rows), :] = upright(col_f[1, 0:1, :])
        send_t(0).wait_recv()
        send_t(1).wait_recv()
        text_half(2, 0)
        send_t(2).wait_recv()
        pl.semaphore_signal(go_sem, inc=1, device_id=sibling, device_id_type=MESH)
        f_1.wait_recv()
        row_c[1] = upright(row_f[1, 0:1, :])

        def near(k):
            send_1(2 * k).wait_recv()

            @pl.when(k == 1)
            def _():
                @pl.when(first)
                def _():
                    pl.semaphore_wait(ready_sem, 2)
                    f_2.start()

                for j in range(PIECES):
                    start_2(j)

            send_1(2 * k + 1).wait_recv()
            image_half(1, k, 0)

        loop(2, near)
        pass_2()
        send_t(3).wait_recv()

        def beside(k):
            text_half(2 + jnp.minimum(k, 1), 1 - k // 2)

            @pl.when(k == 1)
            def _():
                out_1[...] = acc_i[1].astype(jnp.bfloat16)
                loop(PIECES, lambda j: back_1(j).start())

        loop(3, beside)
        f_2.wait_recv()
        row_c[2] = upright(row_f[2, 0:1, :])

        def far(k):
            send_2(2 * k).wait_recv()
            send_2(2 * k + 1).wait_recv()

            def side(g):
                image_half(2, k, 1 - g)

                @pl.when(jnp.logical_and(k == 1, g == 0))
                def _():
                    out_t[...] = acc_t[pl.ds(rows, rows), :].astype(jnp.bfloat16)
                    loop(PIECES, lambda j: back_t(j).start())

            loop(2, side)
            at = pl.ds(pl.multiple_of(k * half, half), half)
            out_2[at, :] = acc_i[2, at, :].astype(jnp.bfloat16)
            for j in range(2):

                @pl.when(k == j)
                def _():
                    start_back(2 * j)
                    start_back(2 * j + 1)

        loop(2, far)

        def near_back(j):
            back_1(j).wait_recv()
            acc_i[0, piece(j), :] += in_1[piece(j), :].astype(jnp.float32)

        loop(PIECES, near_back)

    pass_back()

    def finish(j):
        back_t(j).wait_recv()
        grad_txt[piece(j), :] = acc_t[piece(j), :] + in_t[piece(j), :].astype(jnp.float32)
        back_2(j).wait_recv()
        grad_img[piece(j), :] = acc_i[0, piece(j), :] + in_2[piece(j), :].astype(jnp.float32)

    loop(PIECES, finish)

    f_t.wait_send()
    f_2.wait_send()
    f_1.wait_send()

    def sent(j):
        for copy in (send_t, send_2, send_1, back_t, back_1, back_2):
            copy(j).wait_send()

    loop(PIECES, sent)

    pass_2(done=True)
    pass_back(done=True)


def store(grad_img, grad_txt, img_out, txt_out, sem):
    copies = [
        pltpu.make_async_copy(grad_img, img_out, sem.at[0]),
        pltpu.make_async_copy(grad_txt, txt_out, sem.at[1]),
    ]
    for copy in copies:
        copy.start()
    for copy in copies:
        copy.wait()


def local(n_blk, images, texts, row_lse, col_lse):
    rows, width = images.shape
    scale = 2.0 / math.sqrt(width)
    lse = jnp.stack([row_lse, col_lse]).astype(jnp.float32)
    factors = jnp.exp(LSE_TOP - jnp.repeat(lse, 8, axis=0))
    bf16, f32 = jnp.bfloat16, jnp.float32
    any_spec = pl.BlockSpec(memory_space=pl.ANY)
    hbm_spec = pl.BlockSpec(memory_space=pltpu.HBM)
    vmem_spec = pl.BlockSpec(memory_space=pltpu.VMEM)
    grads = pl.pallas_call(
        functools.partial(kernel, n_blk, scale),
        out_shape=[pltpu.VMEM((rows, width), f32)] * 2,
        in_specs=[hbm_spec, hbm_spec, vmem_spec],
        out_specs=[vmem_spec] * 2,
        scratch_shapes=[
            pltpu.VMEM((2 * rows, width), bf16),
            pltpu.VMEM((3, rows, width), bf16),
            pltpu.VMEM((3, 8, rows), f32),
            pltpu.VMEM((2, 8, rows), f32),
            pltpu.VMEM((3, rows, 128), f32),
            pltpu.VMEM((2 * rows, 128), f32),
            pltpu.VMEM((2 * rows, width), f32),
            pltpu.VMEM((3, rows, width), f32),
        ]
        + [pltpu.VMEM((rows, width), bf16)] * 6
        + [
            pltpu.SemaphoreType.DMA((2,)),
            pltpu.SemaphoreType.DMA((6, PIECES)),
            pltpu.SemaphoreType.DMA((6, PIECES)),
            pltpu.SemaphoreType.DMA((3,)),
            pltpu.SemaphoreType.DMA((3,)),
            pltpu.SemaphoreType.REGULAR,
            pltpu.SemaphoreType.REGULAR,
            pltpu.VMEM((2, max(n for _, _, _, n in ROUTES), width), bf16),
            pltpu.SemaphoreType.DMA((2,)),
            pltpu.SemaphoreType.DMA((2,)),
        ],
        compiler_params=pltpu.CompilerParams(
            collective_id=0, has_side_effects=True, vmem_limit_bytes=48 * 2**20
        ),
        cost_estimate=pl.CostEstimate(
            flops=18 * 2 * rows * rows * width,
            bytes_accessed=12 * rows * width,
            transcendentals=6 * rows * rows,
        ),
        name="contrastive",
    )(
        pltpu.with_memory_space_constraint(texts, pltpu.HBM),
        pltpu.with_memory_space_constraint(images, pltpu.HBM),
        factors,
    )
    return tuple(
        pl.pallas_call(
            store,
            out_shape=[jax.ShapeDtypeStruct((rows, width), f32)] * 2,
            in_specs=[vmem_spec] * 2,
            out_specs=[any_spec] * 2,
            scratch_shapes=[pltpu.SemaphoreType.DMA((2,))],
            compiler_params=pltpu.CompilerParams(vmem_limit_bytes=16 * 2**20),
            name="store",
        )(*grads)
    )


def solution(mesh):
    both = ("blk", "grp")
    return jax.shard_map(
        functools.partial(local, mesh.shape["blk"]),
        mesh=mesh,
        in_specs=(P(both, None), P(both, None), P(both), P(both)),
        out_specs=(P(both, None), P(both, None)),
        check_vma=False,
    )
```

```python
import functools
import math

import jax
import jax.numpy as jnp
from jax import lax
from jax.experimental import pallas as pl
from jax.experimental.pallas import tpu as pltpu
from jax.sharding import PartitionSpec as P

MESH = pl.DeviceIdType.MESH
LSE_TOP = 10.0
LOG2E = math.log2(math.e)
PIECES = 4
NX, NZ = 4, 8
ROUTES_2 = (
    (2, 0, 0, 64),
    (2, 1, 64, 64),
    (0, 0, 128, 64),
    (1, 0, 192, 64),
    (2, 2, 256, 64),
    (2, 3, 320, 64),
    (3, 7, 384, 64),
    (0, 7, 448, 64),
)
ROUTES_BACK = (
    (0, 0, 0, 64),
    (1, 6, 64, 64),
    (1, 2, 128, 64),
    (1, 7, 192, 64),
    (3, 0, 256, 64),
    (1, 5, 320, 64),
    (1, 1, 384, 64),
    (1, 4, 448, 64),
)
RELAY_ROWS = 64
Z_SOON = 1


def kernel(
    n_blk,
    scale,
    texts_in,
    images_in,
    row_lse,
    col_lse,
    grad_img,
    grad_txt,
    txt,
    img,
    row_f,
    col_f,
    row_c,
    col_c,
    acc_t,
    acc_i,
    out_t,
    out_1,
    out_2,
    in_t,
    in_1,
    in_2,
    lse_0,
    lse_1,
    load_sem,
    send_sem,
    recv_sem,
    f_send,
    f_recv,
    go_sem,
    ready_sem,
    relay,
    relay_send,
    relay_recv,
):
    rows = texts_in.shape[0]
    half = rows // 2
    part = rows // PIECES
    c = lax.axis_index("blk")
    h = lax.axis_index("grp")
    core = lax.rem(c, 2)
    other = (c, 1 - h)
    sibling = (c + 1 - 2 * core, h)
    ahead = (lax.rem(c + 2, n_blk), h)
    behind = (lax.rem(c + n_blk - 2, n_blk), h)

    x, z, y = lax.rem(c // 2, NX), lax.rem(c // (2 * NX), NZ), c // (2 * NX * NZ)

    def chip(cx, cz, cy):
        return ((cy * NZ + cz) * NX + cx) * 2 + core, h

    def is_at(cx, cz):
        return jnp.logical_and(x == cx, z == cz)

    first, last = is_at(0, 0), is_at(NX - 1, NZ - 1)

    def piece(j, base=0):
        return pl.ds(pl.multiple_of(base + j * part, part), part)

    def remote(src, dst, sends, recvs, to):
        return pltpu.make_async_remote_copy(
            src_ref=src, dst_ref=dst, send_sem=sends, recv_sem=recvs, device_id=to, device_id_type=MESH
        )

    def remote_k(kind, j, src, dst, to):
        return remote(src, dst, send_sem.at[kind, j], recv_sem.at[kind, j], to)

    def send_t(j):
        return remote_k(0, j, texts_in.at[piece(j)], txt.at[piece(j, rows)], other)

    def send_2(j):
        return remote_k(1, j, images_in.at[piece(j)], img.at[2, piece(j)], behind)

    def send_1(j):
        return remote_k(2, j, images_in.at[piece(j)], img.at[1, piece(j)], sibling)

    def pass_1(j):
        return remote_k(2, j, img.at[2, piece(j)], img.at[1, piece(j)], sibling)

    def back_t(j):
        return remote_k(3, j, out_t.at[piece(j)], in_t.at[piece(j)], other)

    def back_1(j):
        return remote_k(4, j, out_1.at[piece(j)], in_1.at[piece(j)], sibling)

    def back_2(j):
        return remote_k(5, j, out_2.at[piece(j)], in_2.at[piece(j)], ahead)

    def send_on(routes, final, src, dst, kind, slot, j):
        for cx, cz, r, n in routes:
            if r // part != j:
                continue
            sem = send_sem.at[kind, j]
            if (cx, cz) == final:
                copy = remote(src.at[pl.ds(r, n)], dst.at[pl.ds(r, n)], sem, recv_sem.at[kind, j], chip(cx, cz, 1 - y))
            else:
                there = relay.at[slot, pl.ds(0, n)]
                copy = remote(src.at[pl.ds(r, n)], there, sem, relay_recv.at[slot], chip(cx, cz, 1 - y))
            copy.start()

    FIRST, LAST = (0, 0), (NX - 1, NZ - 1)

    def send_routes(j, routes=ROUTES_2):
        send_on(routes, LAST, images_in, img.at[2], 1, 0, j)

    def start_2(j):
        @pl.when(jnp.logical_not(first))
        def _():
            send_2(j).start()

        @pl.when(first)
        def _():
            send_routes(j)

    def start_back(j):
        @pl.when(jnp.logical_not(last))
        def _():
            back_2(j).start()

        @pl.when(last)
        def _():
            send_on(ROUTES_BACK, FIRST, out_2, in_2, 5, 1, j)

    def on_route(routes, final, slot, kind, dst, done):
        for cx, cz, r, n in routes:
            if (cx, cz) == final:
                continue

            @pl.when(is_at(cx, cz))
            def _():
                here = relay.at[slot, pl.ds(0, n)]
                if not done:
                    if slot == 0:
                        pl.semaphore_wait(ready_sem.at[1], 1)
                    remote(here, here, relay_send.at[slot], relay_recv.at[slot], chip(*final, y)).wait_recv()
                copy = remote(here, dst.at[pl.ds(r, n)], relay_send.at[slot], recv_sem.at[kind, r // part], chip(*final, y))
                if done:
                    copy.wait_send()
                else:
                    copy.start()

    def pass_2(done=False):
        on_route(ROUTES_2, LAST, 0, 1, img.at[2], done)

    def pass_back(done=False):
        on_route(ROUTES_BACK, FIRST, 1, 5, in_2, done)

    f_t = remote(col_f.at[0], col_f.at[1], f_send.at[0], f_recv.at[0], other)
    f_2 = remote(row_f.at[0], row_f.at[2], f_send.at[1], f_recv.at[1], behind)
    f_1 = remote(row_f.at[0], row_f.at[1], f_send.at[2], f_recv.at[2], sibling)
    f_1_pass = remote(row_f.at[2], row_f.at[1], f_send.at[2], f_recv.at[2], sibling)

    load_t = pltpu.make_async_copy(texts_in, txt.at[pl.ds(0, rows)], load_sem.at[0])
    load_i = pltpu.make_async_copy(images_in, img.at[0], load_sem.at[1])

    lse = (lse_0, lse_1)
    load_l = [
        pltpu.make_async_copy(row_lse, lse_0, load_sem.at[2]),
        pltpu.make_async_copy(col_lse, lse_1, load_sem.at[3]),
    ]
    for copy in load_l:
        copy.start()

    barrier = pltpu.get_barrier_semaphore()

    def greet(device):
        pl.semaphore_signal(barrier, inc=1, device_id=device, device_id_type=MESH)

    def tell(role, device):
        pl.semaphore_signal(ready_sem.at[role], inc=1, device_id=device, device_id_type=MESH)

    between = [(cx, cz) for cx, cz, _, _ in ROUTES_2 if (cx, cz) != LAST]
    soon = [at for at in between if at[1] <= Z_SOON]
    later = [at for at in between if at[1] > Z_SOON]
    back = [(cx, cz) for cx, cz, _, _ in ROUTES_BACK if (cx, cz) != FIRST]

    for device in (other, sibling, behind):
        greet(device)

    @pl.when(jnp.logical_not(last))
    def _():
        greet(ahead)

    greetings = 4 + jnp.where(first, len(soon) - 1, 0) + jnp.where(last, len(between) + len(back), 0)
    for at in between:

        @pl.when(is_at(*at))
        def _():
            greet(chip(*LAST, y))

    for at in soon:

        @pl.when(is_at(*at))
        def _():
            greet(chip(*FIRST, 1 - y))

    for at in later:
        greetings += jnp.where(is_at(*at), 1, 0)

    for at in back:
        greetings += jnp.where(is_at(*at), 1, 0)

        @pl.when(is_at(*at))
        def _():
            greet(chip(*LAST, 1 - y))

    @pl.when(first)
    def _():
        for at in later:
            greet(chip(*at, 1 - y))
        for at in back:
            greet(chip(*at, y))

    load_t.start()
    load_i.start()
    for k, line in enumerate((row_f, col_f)):
        load_l[k].wait()
        factor = jnp.exp(LSE_TOP - lse[k][...].astype(jnp.float32))
        line[0] = jnp.broadcast_to(factor.reshape(1, rows), (8, rows))
    pl.semaphore_wait(barrier, greetings)

    @pl.when(last)
    def _():
        tell(0, chip(*FIRST, 1 - y))
        for at in between:
            tell(1, chip(*at, y))

    for at in later:

        @pl.when(is_at(*at))
        def _():
            tell(0, chip(*FIRST, 1 - y))

    f_t.start()

    @pl.when(jnp.logical_not(first))
    def _():
        f_2.start()


    @pl.when(core == 0)
    def _():
        @pl.when(jnp.logical_not(first))
        def _():
            for j in range(PIECES):
                send_2(j).start()

        @pl.when(first)
        def _():
            for j in range(PIECES):
                send_routes(j, [route for route in ROUTES_2 if route[:2] in soon])

    @pl.when(core == 1)
    def _():
        f_1.start()
        for j in range(PIECES):
            send_t(j).start()
        for j in range(PIECES):
            send_1(j).start()

    acc_t[...] = jnp.zeros(acc_t.shape, jnp.float32)
    acc_i[...] = jnp.zeros(acc_i.shape, jnp.float32)

    def upright(line):
        return jnp.broadcast_to(line, (128, rows)).T

    col_c[pl.ds(0, rows), :] = upright(col_f[0, 0:1, :])

    def weights(s, upright_f, line_f):
        wide = jnp.concatenate([upright_f] * (s.shape[1] // 128), axis=1)
        return jnp.exp2(s * (scale * LOG2E) - LSE_TOP * LOG2E) * (wide + line_f)

    def scores(a, b):
        return lax.dot_general(a, b, (((1,), (1,)), ((), ())), preferred_element_type=jnp.float32)

    def times(a, b):
        return jnp.dot(a, b, preferred_element_type=jnp.float32)

    def turned_times(a, b):
        return lax.dot_general(a, b, (((0,), (0,)), ((), ())), preferred_element_type=jnp.float32)

    def text_half(k, d, diagonal=False):
        at = pl.ds(pl.multiple_of(k * half, half), half)
        t, i = txt[at, :], img[d]
        w = weights(scores(t, i), col_c[at, :], row_f[d, 0:1, :])
        if diagonal:
            t_id = lax.broadcasted_iota(jnp.int32, w.shape, 0) + k * half
            i_id = lax.broadcasted_iota(jnp.int32, w.shape, 1)
            w = w - jnp.where(t_id == i_id, 2.0, 0.0)
        w = w.astype(jnp.bfloat16)
        acc_t[at, :] += times(w, i)
        acc_i[d] += turned_times(w, t)

    def image_half(d, k, g):
        at = pl.ds(pl.multiple_of(k * half, half), half)
        t_at = pl.ds(pl.multiple_of(g * rows, rows), rows)
        t, i = txt[t_at, :], img[d, at, :]
        w = weights(scores(i, t), row_c[d, at, :], col_f[g, 0:1, :]).astype(jnp.bfloat16)
        acc_i[d, at, :] += times(w, t)
        acc_t[t_at, :] += turned_times(w, i)

    def loop(count, body):
        def step(k, carry):
            body(k)
            return carry

        lax.fori_loop(0, count, step, 0)

    load_t.wait()
    load_i.wait()
    loop(2, lambda k: text_half(k, 0, True))

    @pl.when(core == 0)
    def _():
        def take(j):
            send_2(j).wait_recv()
            pass_1(j).start()

        f_1.wait_recv()
        for j in range(PIECES):
            send_1(j).wait_recv()
        loop(2, lambda k: text_half(k, 1))

        @pl.when(first)
        def _():
            pl.semaphore_wait(ready_sem.at[0], len(later) + 1)
            f_2.start()
            for j in range(PIECES):
                send_routes(j, [route for route in ROUTES_2 if route[:2] not in soon])

        def start_t():
            pl.semaphore_wait(go_sem, 1)
            for j in range(PIECES):
                send_t(j).start()

        pl.when(last)(start_t)
        take(0)
        f_2.wait_recv()
        f_1_pass.start()
        row_c[2] = upright(row_f[2, 0:1, :])

        def both(k):
            @pl.when(k == 0)
            def _():
                take(1)

            @pl.when(k == 1)
            def _():
                pass_2()
                pl.when(jnp.logical_not(last))(start_t)
                take(2)
                take(3)

            image_half(2, k, 0)

        loop(2, both)
        f_t.wait_recv()
        col_c[pl.ds(rows, rows), :] = upright(col_f[1, 0:1, :])
        send_t(0).wait_recv()
        send_t(1).wait_recv()
        loop(3, lambda d: text_half(2, d))
        out_t[pl.ds(0, half), :] = acc_t[pl.ds(rows, half), :].astype(jnp.bfloat16)
        send_t(2).wait_recv()
        send_t(3).wait_recv()
        back_t(0).start()
        back_t(1).start()

        def ending(k):
            text_half(3, 2 - k)

            @pl.when(k == 0)
            def _():
                def on(j):
                    back_1(j).wait_recv()
                    both = acc_i[2, piece(j), :] + in_1[piece(j), :].astype(jnp.float32)
                    out_2[piece(j), :] = both.astype(jnp.bfloat16)
                    start_back(j)

                for j in range(PIECES):
                    on(j)

            @pl.when(k == 1)
            def _():
                out_1[...] = acc_i[1].astype(jnp.bfloat16)
                loop(PIECES, lambda j: back_1(j).start())

        loop(3, ending)
        out_t[pl.ds(half, half), :] = acc_t[pl.ds(rows + half, half), :].astype(jnp.bfloat16)
        back_t(2).start()
        back_t(3).start()

    @pl.when(core == 1)
    def _():
        f_t.wait_recv()
        col_c[pl.ds(rows, rows), :] = upright(col_f[1, 0:1, :])
        send_t(0).wait_recv()
        send_t(1).wait_recv()
        pl.semaphore_signal(go_sem, inc=1, device_id=sibling, device_id_type=MESH)
        text_half(2, 0)
        f_1.wait_recv()
        row_c[1] = upright(row_f[1, 0:1, :])

        def near(k):
            send_1(2 * k).wait_recv()
            send_1(2 * k + 1).wait_recv()

            @pl.when(k == 0)
            def _():
                @pl.when(first)
                def _():
                    pl.semaphore_wait(ready_sem.at[0], len(later) + 1)
                    f_2.start()

                for j in range(PIECES):
                    start_2(j)

            image_half(1, k, 0)

        loop(2, near)
        send_t(2).wait_recv()
        send_t(3).wait_recv()

        def beside(k):
            text_half(2 + jnp.minimum(k, 1), 1 - k // 2)

            @pl.when(k == 1)
            def _():
                out_1[...] = acc_i[1].astype(jnp.bfloat16)
                loop(PIECES, lambda j: back_1(j).start())
                pass_2()

        loop(3, beside)
        f_2.wait_recv()
        row_c[2] = upright(row_f[2, 0:1, :])

        def far(k):
            send_2(2 * k).wait_recv()
            send_2(2 * k + 1).wait_recv()

            def side(g):
                image_half(2, k, 1 - g)

                @pl.when(jnp.logical_and(k == 1, g == 0))
                def _():
                    out_t[...] = acc_t[pl.ds(rows, rows), :].astype(jnp.bfloat16)
                    loop(PIECES, lambda j: back_t(j).start())

            loop(2, side)
            at = pl.ds(pl.multiple_of(k * half, half), half)
            out_2[at, :] = acc_i[2, at, :].astype(jnp.bfloat16)
            for j in range(2):

                @pl.when(k == j)
                def _():
                    start_back(2 * j)
                    start_back(2 * j + 1)

        loop(2, far)

        def near_back(j):
            back_1(j).wait_recv()
            acc_i[0, piece(j), :] += in_1[piece(j), :].astype(jnp.float32)

        loop(PIECES, near_back)

    pass_back()

    def finish(j):
        back_t(j).wait_recv()
        grad_txt[piece(j), :] = acc_t[piece(j), :] + in_t[piece(j), :].astype(jnp.float32)
        back_2(j).wait_recv()
        grad_img[piece(j), :] = acc_i[0, piece(j), :] + in_2[piece(j), :].astype(jnp.float32)

    loop(PIECES, finish)

    f_t.wait_send()
    f_2.wait_send()
    f_1.wait_send()

    def sent(j):
        for copy in (send_t, send_2, send_1, back_t, back_1, back_2):
            copy(j).wait_send()

    loop(PIECES, sent)

    pass_2(done=True)
    pass_back(done=True)


def store(grad_img, grad_txt, img_out, txt_out, sem):
    rows = grad_img.shape[0] // PIECES
    copies = []
    for j in range(PIECES):
        for k, (src, dst) in enumerate(((grad_img, img_out), (grad_txt, txt_out))):
            at = pl.ds(j * rows, rows)
            copies.append(pltpu.make_async_copy(src.at[at], dst.at[at], sem.at[k, j]))
    for copy in copies:
        copy.start()
    for copy in copies:
        copy.wait()


def local(n_blk, images, texts, row_lse, col_lse):
    rows, width = images.shape
    scale = 2.0 / math.sqrt(width)
    bf16, f32 = jnp.bfloat16, jnp.float32
    any_spec = pl.BlockSpec(memory_space=pl.ANY)
    hbm_spec = pl.BlockSpec(memory_space=pltpu.HBM)
    vmem_spec = pl.BlockSpec(memory_space=pltpu.VMEM)
    grads = pl.pallas_call(
        functools.partial(kernel, n_blk, scale),
        out_shape=[pltpu.VMEM((rows, width), f32)] * 2,
        in_specs=[hbm_spec] * 4,
        out_specs=[vmem_spec] * 2,
        scratch_shapes=[
            pltpu.VMEM((2 * rows, width), bf16),
            pltpu.VMEM((3, rows, width), bf16),
            pltpu.VMEM((3, 8, rows), f32),
            pltpu.VMEM((2, 8, rows), f32),
            pltpu.VMEM((3, rows, 128), f32),
            pltpu.VMEM((2 * rows, 128), f32),
            pltpu.VMEM((2 * rows, width), f32),
            pltpu.VMEM((3, rows, width), f32),
        ]
        + [pltpu.VMEM((rows, width), bf16)] * 6
        + [
            pltpu.VMEM((rows,), bf16),
            pltpu.VMEM((rows,), bf16),
            pltpu.SemaphoreType.DMA((4,)),
            pltpu.SemaphoreType.DMA((6, PIECES)),
            pltpu.SemaphoreType.DMA((6, PIECES)),
            pltpu.SemaphoreType.DMA((3,)),
            pltpu.SemaphoreType.DMA((3,)),
            pltpu.SemaphoreType.REGULAR,
            pltpu.SemaphoreType.REGULAR((2,)),
            pltpu.VMEM((2, RELAY_ROWS, width), bf16),
            pltpu.SemaphoreType.DMA((2,)),
            pltpu.SemaphoreType.DMA((2,)),
        ],
        compiler_params=pltpu.CompilerParams(
            collective_id=0, has_side_effects=True, vmem_limit_bytes=48 * 2**20
        ),
        cost_estimate=pl.CostEstimate(
            flops=18 * 2 * rows * rows * width,
            bytes_accessed=12 * rows * width,
            transcendentals=6 * rows * rows,
        ),
        name="contrastive",
    )(
        pltpu.with_memory_space_constraint(texts, pltpu.HBM),
        pltpu.with_memory_space_constraint(images, pltpu.HBM),
        pltpu.with_memory_space_constraint(row_lse, pltpu.HBM),
        pltpu.with_memory_space_constraint(col_lse, pltpu.HBM),
    )
    return tuple(
        pl.pallas_call(
            store,
            out_shape=[jax.ShapeDtypeStruct((rows, width), f32)] * 2,
            in_specs=[vmem_spec] * 2,
            out_specs=[any_spec] * 2,
            scratch_shapes=[pltpu.SemaphoreType.DMA((2, PIECES))],
            compiler_params=pltpu.CompilerParams(vmem_limit_bytes=16 * 2**20),
            name="store",
        )(*grads)
    )


def solution(mesh):
    both = ("blk", "grp")
    return jax.shard_map(
        functools.partial(local, mesh.shape["blk"]),
        mesh=mesh,
        in_specs=(P(both, None), P(both, None), P(both), P(both)),
        out_specs=(P(both, None), P(both, None)),
        check_vma=False,
    )
```

```python
import functools
import math

import jax
import jax.numpy as jnp
from jax import lax
from jax.experimental import pallas as pl
from jax.experimental.pallas import tpu as pltpu
from jax.sharding import PartitionSpec as P

MESH = pl.DeviceIdType.MESH
LSE_TOP = 10.0
LOG2E = math.log2(math.e)
PIECES = 4
NX, NZ = 4, 8
ROUTES_2 = (
    (2, 0, 0, 64),
    (2, 1, 64, 64),
    (0, 0, 128, 64),
    (1, 0, 192, 64),
    (1, 1, 256, 64),
    (2, 2, 320, 64),
    (2, 3, 384, 64),
    (0, 7, 448, 64),
)
ROUTES_BACK = (
    (0, 0, 0, 64),
    (1, 6, 64, 64),
    (1, 7, 128, 64),
    (1, 5, 192, 64),
    (3, 0, 256, 64),
    (1, 4, 320, 64),
    (2, 7, 384, 64),
    (2, 0, 448, 64),
)
RELAY_ROWS = 64
Z_SOON, Z_MID = 1, 3


def kernel(
    n_blk,
    scale,
    texts_in,
    images_in,
    row_lse,
    col_lse,
    grad_img,
    grad_txt,
    txt,
    img,
    row_f,
    col_f,
    row_c,
    col_c,
    acc_t,
    acc_i,
    out_t,
    out_1,
    out_2,
    in_t,
    in_1,
    in_2,
    lse_0,
    lse_1,
    load_sem,
    send_sem,
    recv_sem,
    f_send,
    f_recv,
    go_sem,
    ready_sem,
    relay,
    relay_send,
    relay_recv,
):
    rows = texts_in.shape[0]
    half = rows // 2
    part = rows // PIECES
    c = lax.axis_index("blk")
    h = lax.axis_index("grp")
    core = lax.rem(c, 2)
    other = (c, 1 - h)
    sibling = (c + 1 - 2 * core, h)
    ahead = (lax.rem(c + 2, n_blk), h)
    behind = (lax.rem(c + n_blk - 2, n_blk), h)

    x, z, y = lax.rem(c // 2, NX), lax.rem(c // (2 * NX), NZ), c // (2 * NX * NZ)

    def chip(cx, cz, cy):
        return ((cy * NZ + cz) * NX + cx) * 2 + core, h

    def is_at(cx, cz):
        return jnp.logical_and(x == cx, z == cz)

    first, last = is_at(0, 0), is_at(NX - 1, NZ - 1)

    def piece(j, base=0):
        return pl.ds(pl.multiple_of(base + j * part, part), part)

    def remote(src, dst, sends, recvs, to):
        return pltpu.make_async_remote_copy(
            src_ref=src, dst_ref=dst, send_sem=sends, recv_sem=recvs, device_id=to, device_id_type=MESH
        )

    def remote_k(kind, j, src, dst, to):
        return remote(src, dst, send_sem.at[kind, j], recv_sem.at[kind, j], to)

    def send_t(j):
        return remote_k(0, j, texts_in.at[piece(j)], txt.at[piece(j, rows)], other)

    def send_2(j):
        return remote_k(1, j, images_in.at[piece(j)], img.at[2, piece(j)], behind)

    def send_1(j):
        return remote_k(2, j, images_in.at[piece(j)], img.at[1, piece(j)], sibling)

    def pass_1(j):
        return remote_k(2, j, img.at[2, piece(j)], img.at[1, piece(j)], sibling)

    def back_t(j):
        return remote_k(3, j, out_t.at[piece(j)], in_t.at[piece(j)], other)

    def back_1(j):
        return remote_k(4, j, out_1.at[piece(j)], in_1.at[piece(j)], sibling)

    def back_2(j):
        return remote_k(5, j, out_2.at[piece(j)], in_2.at[piece(j)], ahead)

    def send_on(routes, final, src, dst, kind, slot, j):
        for cx, cz, r, n in routes:
            if r // part != j:
                continue
            sem = send_sem.at[kind, j]
            if (cx, cz) == final:
                copy = remote(src.at[pl.ds(r, n)], dst.at[pl.ds(r, n)], sem, recv_sem.at[kind, j], chip(cx, cz, 1 - y))
            else:
                there = relay.at[slot, pl.ds(0, n)]
                copy = remote(src.at[pl.ds(r, n)], there, sem, relay_recv.at[slot], chip(cx, cz, 1 - y))
            copy.start()

    FIRST, LAST = (0, 0), (NX - 1, NZ - 1)

    def send_routes(j, routes=ROUTES_2):
        send_on(routes, LAST, images_in, img.at[2], 1, 0, j)

    def start_2(j):
        @pl.when(jnp.logical_not(first))
        def _():
            send_2(j).start()

        @pl.when(first)
        def _():
            send_routes(j)

    def start_back(j):
        @pl.when(jnp.logical_not(last))
        def _():
            back_2(j).start()

        @pl.when(last)
        def _():
            send_on(ROUTES_BACK, FIRST, out_2, in_2, 5, 1, j)

    def on_route(routes, final, slot, kind, dst, done):
        for cx, cz, r, n in routes:
            if (cx, cz) == final:
                continue

            @pl.when(is_at(cx, cz))
            def _():
                here = relay.at[slot, pl.ds(0, n)]
                if not done:
                    if slot == 0:
                        pl.semaphore_wait(ready_sem.at[1], 1)
                    remote(here, here, relay_send.at[slot], relay_recv.at[slot], chip(*final, y)).wait_recv()
                copy = remote(here, dst.at[pl.ds(r, n)], relay_send.at[slot], recv_sem.at[kind, r // part], chip(*final, y))
                if done:
                    copy.wait_send()
                else:
                    copy.start()

    def pass_2(done=False):
        on_route(ROUTES_2, LAST, 0, 1, img.at[2], done)

    def pass_back(done=False):
        on_route(ROUTES_BACK, FIRST, 1, 5, in_2, done)

    f_t = remote(col_f.at[0], col_f.at[1], f_send.at[0], f_recv.at[0], other)
    f_2 = remote(row_f.at[0], row_f.at[2], f_send.at[1], f_recv.at[1], behind)
    f_1 = remote(row_f.at[0], row_f.at[1], f_send.at[2], f_recv.at[2], sibling)
    f_1_pass = remote(row_f.at[2], row_f.at[1], f_send.at[2], f_recv.at[2], sibling)

    load_t = pltpu.make_async_copy(texts_in, txt.at[pl.ds(0, rows)], load_sem.at[0])
    load_i = pltpu.make_async_copy(images_in, img.at[0], load_sem.at[1])

    lse = (lse_0, lse_1)
    load_l = [
        pltpu.make_async_copy(row_lse, lse_0, load_sem.at[2]),
        pltpu.make_async_copy(col_lse, lse_1, load_sem.at[3]),
    ]
    for copy in load_l:
        copy.start()

    barrier = pltpu.get_barrier_semaphore()

    def greet(device):
        pl.semaphore_signal(barrier, inc=1, device_id=device, device_id_type=MESH)

    def tell(role, device):
        pl.semaphore_signal(ready_sem.at[role], inc=1, device_id=device, device_id_type=MESH)

    between = [(cx, cz) for cx, cz, _, _ in ROUTES_2 if (cx, cz) != LAST]
    soon = [at for at in between if at[1] <= Z_SOON]
    mid = [at for at in between if Z_SOON < at[1] <= Z_MID]
    later = [at for at in between if at[1] > Z_MID]
    back = [(cx, cz) for cx, cz, _, _ in ROUTES_BACK if (cx, cz) != FIRST]

    for device in (other, sibling, behind):
        greet(device)

    @pl.when(jnp.logical_not(last))
    def _():
        greet(ahead)

    greetings = 4 + jnp.where(first, len(soon) - 1, 0) + jnp.where(last, len(between) + len(back), 0)
    for at in between:

        @pl.when(is_at(*at))
        def _():
            greet(chip(*LAST, y))

    for at in soon:

        @pl.when(is_at(*at))
        def _():
            greet(chip(*FIRST, 1 - y))

    for at in mid + later:
        greetings += jnp.where(is_at(*at), 1, 0)

    for at in back:
        greetings += jnp.where(is_at(*at), 1, 0)

        @pl.when(is_at(*at))
        def _():
            greet(chip(*LAST, 1 - y))

    @pl.when(first)
    def _():
        for at in mid + later:
            greet(chip(*at, 1 - y))
        for at in back:
            greet(chip(*at, y))

    load_t.start()
    load_i.start()
    for k, line in enumerate((row_f, col_f)):
        load_l[k].wait()
        factor = jnp.exp(LSE_TOP - lse[k][...].astype(jnp.float32))
        line[0] = jnp.broadcast_to(factor.reshape(1, rows), (8, rows))
    pl.semaphore_wait(barrier, greetings)

    @pl.when(last)
    def _():
        tell(0, chip(*FIRST, 1 - y))
        for at in between:
            tell(1, chip(*at, y))

    for at in mid + later:

        @pl.when(is_at(*at))
        def _():
            tell(2 if at in mid else 0, chip(*FIRST, 1 - y))

    f_t.start()

    @pl.when(jnp.logical_not(first))
    def _():
        f_2.start()


    @pl.when(core == 0)
    def _():
        @pl.when(jnp.logical_not(first))
        def _():
            for j in range(PIECES):
                send_2(j).start()

        @pl.when(first)
        def _():
            for j in range(PIECES):
                send_routes(j, [route for route in ROUTES_2 if route[:2] in soon])

    @pl.when(core == 1)
    def _():
        f_1.start()
        for j in range(PIECES):
            send_t(j).start()
        for j in range(PIECES):
            send_1(j).start()

    acc_t[...] = jnp.zeros(acc_t.shape, jnp.float32)
    acc_i[...] = jnp.zeros(acc_i.shape, jnp.float32)

    def upright(line):
        return jnp.broadcast_to(line, (128, rows)).T

    col_c[pl.ds(0, rows), :] = upright(col_f[0, 0:1, :])

    def weights(s, upright_f, line_f):
        wide = jnp.concatenate([upright_f] * (s.shape[1] // 128), axis=1)
        return jnp.exp2(s * (scale * LOG2E) - LSE_TOP * LOG2E) * (wide + line_f)

    def scores(a, b):
        return lax.dot_general(a, b, (((1,), (1,)), ((), ())), preferred_element_type=jnp.float32)

    def times(a, b):
        return jnp.dot(a, b, preferred_element_type=jnp.float32)

    def turned_times(a, b):
        return lax.dot_general(a, b, (((0,), (0,)), ((), ())), preferred_element_type=jnp.float32)

    def text_half(k, d, diagonal=False):
        at = pl.ds(pl.multiple_of(k * half, half), half)
        t, i = txt[at, :], img[d]
        w = weights(scores(t, i), col_c[at, :], row_f[d, 0:1, :])
        if diagonal:
            t_id = lax.broadcasted_iota(jnp.int32, w.shape, 0) + k * half
            i_id = lax.broadcasted_iota(jnp.int32, w.shape, 1)
            w = w - jnp.where(t_id == i_id, 2.0, 0.0)
        w = w.astype(jnp.bfloat16)
        acc_t[at, :] += times(w, i)
        acc_i[d] += turned_times(w, t)

    def image_half(d, k, g):
        at = pl.ds(pl.multiple_of(k * half, half), half)
        t_at = pl.ds(pl.multiple_of(g * rows, rows), rows)
        t, i = txt[t_at, :], img[d, at, :]
        w = weights(scores(i, t), row_c[d, at, :], col_f[g, 0:1, :]).astype(jnp.bfloat16)
        acc_i[d, at, :] += times(w, t)
        acc_t[t_at, :] += turned_times(w, i)

    def loop(count, body):
        def step(k, carry):
            body(k)
            return carry

        lax.fori_loop(0, count, step, 0)

    load_t.wait()
    load_i.wait()
    loop(2, lambda k: text_half(k, 0, True))

    @pl.when(core == 0)
    def _():
        def take(j):
            send_2(j).wait_recv()
            pass_1(j).start()

        @pl.when(first)
        def _():
            pl.semaphore_wait(ready_sem.at[2], len(mid))
            for j in range(PIECES):
                send_routes(j, [route for route in ROUTES_2 if route[:2] in mid])

        f_1.wait_recv()
        for j in range(PIECES):
            send_1(j).wait_recv()
        loop(2, lambda k: text_half(k, 1))

        @pl.when(first)
        def _():
            pl.semaphore_wait(ready_sem.at[0], len(later) + 1)
            f_2.start()
            for j in range(PIECES):
                send_routes(j, [route for route in ROUTES_2 if route[:2] in later])

        def start_t():
            pl.semaphore_wait(go_sem, 1)
            for j in range(PIECES):
                send_t(j).start()

        pl.when(last)(start_t)
        take(0)
        f_2.wait_recv()
        f_1_pass.start()
        row_c[2] = upright(row_f[2, 0:1, :])

        def both(k):
            @pl.when(k == 0)
            def _():
                take(1)

            @pl.when(k == 1)
            def _():
                pass_2()
                pl.when(jnp.logical_not(last))(start_t)
                take(2)
                take(3)

            image_half(2, k, 0)

        loop(2, both)
        f_t.wait_recv()
        col_c[pl.ds(rows, rows), :] = upright(col_f[1, 0:1, :])
        send_t(0).wait_recv()
        send_t(1).wait_recv()
        loop(3, lambda d: text_half(2, d))
        out_t[pl.ds(0, half), :] = acc_t[pl.ds(rows, half), :].astype(jnp.bfloat16)
        send_t(2).wait_recv()
        send_t(3).wait_recv()
        back_t(0).start()
        back_t(1).start()

        def ending(k):
            text_half(3, 2 - k)

            @pl.when(k == 0)
            def _():
                def on(j):
                    back_1(j).wait_recv()
                    both = acc_i[2, piece(j), :] + in_1[piece(j), :].astype(jnp.float32)
                    out_2[piece(j), :] = both.astype(jnp.bfloat16)
                    start_back(j)

                for j in range(PIECES):
                    on(j)

            @pl.when(k == 1)
            def _():
                out_1[...] = acc_i[1].astype(jnp.bfloat16)
                loop(PIECES, lambda j: back_1(j).start())

        loop(3, ending)
        out_t[pl.ds(half, half), :] = acc_t[pl.ds(rows + half, half), :].astype(jnp.bfloat16)
        back_t(2).start()
        back_t(3).start()

    @pl.when(core == 1)
    def _():
        f_t.wait_recv()
        col_c[pl.ds(rows, rows), :] = upright(col_f[1, 0:1, :])
        send_t(0).wait_recv()
        send_t(1).wait_recv()
        pl.semaphore_signal(go_sem, inc=1, device_id=sibling, device_id_type=MESH)
        text_half(2, 0)
        f_1.wait_recv()
        row_c[1] = upright(row_f[1, 0:1, :])

        def near(k):
            send_1(2 * k).wait_recv()
            send_1(2 * k + 1).wait_recv()

            @pl.when(k == 0)
            def _():
                @pl.when(first)
                def _():
                    pl.semaphore_wait(ready_sem.at[2], len(mid))
                    pl.semaphore_wait(ready_sem.at[0], len(later) + 1)
                    f_2.start()

                for j in range(PIECES):
                    start_2(j)

            image_half(1, k, 0)

        loop(2, near)
        send_t(2).wait_recv()
        send_t(3).wait_recv()

        def beside(k):
            text_half(2 + jnp.minimum(k, 1), 1 - k // 2)

            @pl.when(k == 1)
            def _():
                out_1[...] = acc_i[1].astype(jnp.bfloat16)
                loop(PIECES, lambda j: back_1(j).start())
                pass_2()

        loop(3, beside)
        f_2.wait_recv()
        row_c[2] = upright(row_f[2, 0:1, :])

        def far(k):
            send_2(2 * k).wait_recv()
            send_2(2 * k + 1).wait_recv()

            def side(g):
                image_half(2, k, 1 - g)

                @pl.when(jnp.logical_and(k == 1, g == 0))
                def _():
                    out_t[...] = acc_t[pl.ds(rows, rows), :].astype(jnp.bfloat16)
                    loop(PIECES, lambda j: back_t(j).start())

            loop(2, side)
            at = pl.ds(pl.multiple_of(k * half, half), half)
            out_2[at, :] = acc_i[2, at, :].astype(jnp.bfloat16)
            for j in range(2):

                @pl.when(k == j)
                def _():
                    start_back(2 * j)
                    start_back(2 * j + 1)

        loop(2, far)

        def near_back(j):
            back_1(j).wait_recv()
            acc_i[0, piece(j), :] += in_1[piece(j), :].astype(jnp.float32)

        loop(PIECES, near_back)

    pass_back()

    def finish(j):
        back_t(j).wait_recv()
        grad_txt[piece(j), :] = acc_t[piece(j), :] + in_t[piece(j), :].astype(jnp.float32)
        back_2(j).wait_recv()
        grad_img[piece(j), :] = acc_i[0, piece(j), :] + in_2[piece(j), :].astype(jnp.float32)

    loop(PIECES, finish)

    f_t.wait_send()
    f_2.wait_send()
    f_1.wait_send()

    def sent(j):
        for copy in (send_t, send_2, send_1, back_t, back_1, back_2):
            copy(j).wait_send()

    loop(PIECES, sent)

    pass_2(done=True)
    pass_back(done=True)


def store(grad_img, grad_txt, img_out, txt_out, sem):
    rows = grad_img.shape[0] // PIECES
    copies = []
    for j in range(PIECES):
        for k, (src, dst) in enumerate(((grad_img, img_out), (grad_txt, txt_out))):
            at = pl.ds(j * rows, rows)
            copies.append(pltpu.make_async_copy(src.at[at], dst.at[at], sem.at[k, j]))
    for copy in copies:
        copy.start()
    for copy in copies:
        copy.wait()


def local(n_blk, images, texts, row_lse, col_lse):
    rows, width = images.shape
    scale = 2.0 / math.sqrt(width)
    bf16, f32 = jnp.bfloat16, jnp.float32
    any_spec = pl.BlockSpec(memory_space=pl.ANY)
    hbm_spec = pl.BlockSpec(memory_space=pltpu.HBM)
    vmem_spec = pl.BlockSpec(memory_space=pltpu.VMEM)
    grads = pl.pallas_call(
        functools.partial(kernel, n_blk, scale),
        out_shape=[pltpu.VMEM((rows, width), f32)] * 2,
        in_specs=[hbm_spec] * 4,
        out_specs=[vmem_spec] * 2,
        scratch_shapes=[
            pltpu.VMEM((2 * rows, width), bf16),
            pltpu.VMEM((3, rows, width), bf16),
            pltpu.VMEM((3, 8, rows), f32),
            pltpu.VMEM((2, 8, rows), f32),
            pltpu.VMEM((3, rows, 128), f32),
            pltpu.VMEM((2 * rows, 128), f32),
            pltpu.VMEM((2 * rows, width), f32),
            pltpu.VMEM((3, rows, width), f32),
        ]
        + [pltpu.VMEM((rows, width), bf16)] * 6
        + [
            pltpu.VMEM((rows,), bf16),
            pltpu.VMEM((rows,), bf16),
            pltpu.SemaphoreType.DMA((4,)),
            pltpu.SemaphoreType.DMA((6, PIECES)),
            pltpu.SemaphoreType.DMA((6, PIECES)),
            pltpu.SemaphoreType.DMA((3,)),
            pltpu.SemaphoreType.DMA((3,)),
            pltpu.SemaphoreType.REGULAR,
            pltpu.SemaphoreType.REGULAR((3,)),
            pltpu.VMEM((2, RELAY_ROWS, width), bf16),
            pltpu.SemaphoreType.DMA((2,)),
            pltpu.SemaphoreType.DMA((2,)),
        ],
        compiler_params=pltpu.CompilerParams(
            collective_id=0, has_side_effects=True, vmem_limit_bytes=48 * 2**20
        ),
        cost_estimate=pl.CostEstimate(
            flops=18 * 2 * rows * rows * width,
            bytes_accessed=12 * rows * width,
            transcendentals=6 * rows * rows,
        ),
        name="contrastive",
    )(
        pltpu.with_memory_space_constraint(texts, pltpu.HBM),
        pltpu.with_memory_space_constraint(images, pltpu.HBM),
        pltpu.with_memory_space_constraint(row_lse, pltpu.HBM),
        pltpu.with_memory_space_constraint(col_lse, pltpu.HBM),
    )
    return tuple(
        pl.pallas_call(
            store,
            out_shape=[jax.ShapeDtypeStruct((rows, width), f32)] * 2,
            in_specs=[vmem_spec] * 2,
            out_specs=[any_spec] * 2,
            scratch_shapes=[pltpu.SemaphoreType.DMA((2, PIECES))],
            compiler_params=pltpu.CompilerParams(vmem_limit_bytes=16 * 2**20),
            name="store",
        )(*grads)
    )


def solution(mesh):
    both = ("blk", "grp")
    return jax.shard_map(
        functools.partial(local, mesh.shape["blk"]),
        mesh=mesh,
        in_specs=(P(both, None), P(both, None), P(both), P(both)),
        out_specs=(P(both, None), P(both, None)),
        check_vma=False,
    )
```

```python
import functools
import math

import jax
import jax.numpy as jnp
from jax import lax
from jax.experimental import pallas as pl
from jax.experimental.pallas import tpu as pltpu
from jax.sharding import PartitionSpec as P

MESH = pl.DeviceIdType.MESH
LSE_TOP = 10.0
LOG2E = math.log2(math.e)
PIECES = 4
NX, NZ = 4, 8
ROUTES_2 = (
    (2, 0, 0, 64),
    (2, 1, 64, 64),
    (1, 0, 128, 64),
    (1, 1, 192, 64),
    (2, 2, 256, 64),
    (2, 3, 320, 64),
    (0, 7, 384, 64),
    (2, 4, 448, 64),
)
ROUTES_BACK = (
    (3, 0, 0, 64),
    (1, 6, 64, 64),
    (1, 7, 128, 64),
    (1, 5, 192, 64),
    (0, 0, 256, 64),
    (1, 4, 320, 64),
    (2, 0, 384, 64),
    (1, 3, 448, 64),
)
RELAY_ROWS = 64
Z_SOON, Z_MID = 1, 3


def kernel(
    n_blk,
    scale,
    texts_in,
    images_in,
    row_lse,
    col_lse,
    grad_img,
    grad_txt,
    txt,
    img,
    row_f,
    col_f,
    row_c,
    col_c,
    acc_t,
    acc_i,
    out_t,
    out_1,
    out_2,
    in_t,
    in_1,
    in_2,
    lse_0,
    lse_1,
    load_sem,
    send_sem,
    recv_sem,
    f_send,
    f_recv,
    go_sem,
    ready_sem,
    relay,
    relay_send,
    relay_recv,
):
    rows = texts_in.shape[0]
    half = rows // 2
    part = rows // PIECES
    c = lax.axis_index("blk")
    h = lax.axis_index("grp")
    core = lax.rem(c, 2)
    other = (c, 1 - h)
    sibling = (c + 1 - 2 * core, h)
    ahead = (lax.rem(c + 2, n_blk), h)
    behind = (lax.rem(c + n_blk - 2, n_blk), h)

    x, z, y = lax.rem(c // 2, NX), lax.rem(c // (2 * NX), NZ), c // (2 * NX * NZ)

    def chip(cx, cz, cy):
        return ((cy * NZ + cz) * NX + cx) * 2 + core, h

    def is_at(cx, cz):
        return jnp.logical_and(x == cx, z == cz)

    first, last = is_at(0, 0), is_at(NX - 1, NZ - 1)

    def piece(j, base=0):
        return pl.ds(pl.multiple_of(base + j * part, part), part)

    def remote(src, dst, sends, recvs, to):
        return pltpu.make_async_remote_copy(
            src_ref=src, dst_ref=dst, send_sem=sends, recv_sem=recvs, device_id=to, device_id_type=MESH
        )

    def remote_k(kind, j, src, dst, to):
        return remote(src, dst, send_sem.at[kind, j], recv_sem.at[kind, j], to)

    def send_t(j):
        return remote_k(0, j, texts_in.at[piece(j)], txt.at[piece(j, rows)], other)

    def send_2(j):
        return remote_k(1, j, images_in.at[piece(j)], img.at[2, piece(j)], behind)

    def send_1(j):
        return remote_k(2, j, images_in.at[piece(j)], img.at[1, piece(j)], sibling)

    def pass_1(j):
        return remote_k(2, j, img.at[2, piece(j)], img.at[1, piece(j)], sibling)

    def back_t(j):
        return remote_k(3, j, out_t.at[piece(j)], in_t.at[piece(j)], other)

    def back_1(j):
        return remote_k(4, j, out_1.at[piece(j)], in_1.at[piece(j)], sibling)

    def back_2(j):
        return remote_k(5, j, out_2.at[piece(j)], in_2.at[piece(j)], ahead)

    def send_on(routes, final, src, dst, kind, slot, j):
        for cx, cz, r, n in routes:
            if r // part != j:
                continue
            sem = send_sem.at[kind, j]
            if (cx, cz) == final:
                copy = remote(src.at[pl.ds(r, n)], dst.at[pl.ds(r, n)], sem, recv_sem.at[kind, j], chip(cx, cz, 1 - y))
            else:
                there = relay.at[slot, pl.ds(0, n)]
                copy = remote(src.at[pl.ds(r, n)], there, sem, relay_recv.at[slot], chip(cx, cz, 1 - y))
            copy.start()

    FIRST, LAST = (0, 0), (NX - 1, NZ - 1)

    def send_routes(j, routes=ROUTES_2):
        send_on(routes, LAST, images_in, img.at[2], 1, 0, j)

    def start_2(j):
        @pl.when(jnp.logical_not(first))
        def _():
            send_2(j).start()

        @pl.when(first)
        def _():
            send_routes(j)

    def start_back(j):
        @pl.when(jnp.logical_not(last))
        def _():
            back_2(j).start()

        @pl.when(last)
        def _():
            send_on(ROUTES_BACK, FIRST, out_2, in_2, 5, 1, j)

    def on_route(routes, final, slot, kind, dst, done):
        for cx, cz, r, n in routes:
            if (cx, cz) == final:
                continue

            @pl.when(is_at(cx, cz))
            def _():
                here = relay.at[slot, pl.ds(0, n)]
                if not done:
                    if slot == 0:
                        pl.semaphore_wait(ready_sem.at[1], 1)
                    remote(here, here, relay_send.at[slot], relay_recv.at[slot], chip(*final, y)).wait_recv()
                copy = remote(here, dst.at[pl.ds(r, n)], relay_send.at[slot], recv_sem.at[kind, r // part], chip(*final, y))
                if done:
                    copy.wait_send()
                else:
                    copy.start()

    def pass_2(done=False):
        on_route(ROUTES_2, LAST, 0, 1, img.at[2], done)

    def pass_back(done=False):
        on_route(ROUTES_BACK, FIRST, 1, 5, in_2, done)

    f_t = remote(col_f.at[0], col_f.at[1], f_send.at[0], f_recv.at[0], other)
    f_2 = remote(row_f.at[0], row_f.at[2], f_send.at[1], f_recv.at[1], behind)
    f_1 = remote(row_f.at[0], row_f.at[1], f_send.at[2], f_recv.at[2], sibling)
    f_1_pass = remote(row_f.at[2], row_f.at[1], f_send.at[2], f_recv.at[2], sibling)

    load_t = pltpu.make_async_copy(texts_in, txt.at[pl.ds(0, rows)], load_sem.at[0])
    load_i = pltpu.make_async_copy(images_in, img.at[0], load_sem.at[1])

    lse = (lse_0, lse_1)
    load_l = [
        pltpu.make_async_copy(row_lse, lse_0, load_sem.at[2]),
        pltpu.make_async_copy(col_lse, lse_1, load_sem.at[3]),
    ]
    for copy in load_l:
        copy.start()

    barrier = pltpu.get_barrier_semaphore()

    def greet(device):
        pl.semaphore_signal(barrier, inc=1, device_id=device, device_id_type=MESH)

    def tell(role, device):
        pl.semaphore_signal(ready_sem.at[role], inc=1, device_id=device, device_id_type=MESH)

    between = [(cx, cz) for cx, cz, _, _ in ROUTES_2 if (cx, cz) != LAST]
    soon = [at for at in between if at[1] <= Z_SOON]
    mid = [at for at in between if Z_SOON < at[1] <= Z_MID]
    later = [at for at in between if at[1] > Z_MID]
    back = [(cx, cz) for cx, cz, _, _ in ROUTES_BACK if (cx, cz) != FIRST]

    for device in (other, sibling, behind):
        greet(device)

    @pl.when(jnp.logical_not(last))
    def _():
        greet(ahead)

    greetings = 4 + jnp.where(first, len(soon) - 1, 0) + jnp.where(last, len(between) + len(back), 0)
    for at in between:

        @pl.when(is_at(*at))
        def _():
            greet(chip(*LAST, y))

    for at in soon:

        @pl.when(is_at(*at))
        def _():
            greet(chip(*FIRST, 1 - y))

    for at in mid + later:
        greetings += jnp.where(is_at(*at), 1, 0)

    for at in back:
        greetings += jnp.where(is_at(*at), 1, 0)

        @pl.when(is_at(*at))
        def _():
            greet(chip(*LAST, 1 - y))

    @pl.when(first)
    def _():
        for at in mid + later:
            greet(chip(*at, 1 - y))
        for at in back:
            greet(chip(*at, y))

    load_t.start()
    load_i.start()
    for k, line in enumerate((row_f, col_f)):
        load_l[k].wait()
        factor = jnp.exp(LSE_TOP - lse[k][...].astype(jnp.float32))
        line[0] = jnp.broadcast_to(factor.reshape(1, rows), (8, rows))
    pl.semaphore_wait(barrier, greetings)

    @pl.when(last)
    def _():
        tell(0, chip(*FIRST, 1 - y))
        for at in between:
            tell(1, chip(*at, y))

    for at in mid + later:

        @pl.when(is_at(*at))
        def _():
            tell(2 if at in mid else 0, chip(*FIRST, 1 - y))

    f_t.start()

    @pl.when(jnp.logical_not(first))
    def _():
        f_2.start()


    @pl.when(core == 0)
    def _():
        @pl.when(jnp.logical_not(first))
        def _():
            for j in range(PIECES):
                send_2(j).start()

        @pl.when(first)
        def _():
            for j in range(PIECES):
                send_routes(j, [route for route in ROUTES_2 if route[:2] in soon])

    @pl.when(core == 1)
    def _():
        f_1.start()
        for j in range(PIECES):
            send_t(j).start()
        for j in range(PIECES):
            send_1(j).start()

    acc_t[...] = jnp.zeros(acc_t.shape, jnp.float32)
    acc_i[...] = jnp.zeros(acc_i.shape, jnp.float32)

    def upright(line):
        return jnp.broadcast_to(line, (128, rows)).T

    col_c[pl.ds(0, rows), :] = upright(col_f[0, 0:1, :])

    def weights(s, upright_f, line_f):
        wide = jnp.concatenate([upright_f] * (s.shape[1] // 128), axis=1)
        return jnp.exp2(s * (scale * LOG2E) - LSE_TOP * LOG2E) * (wide + line_f)

    def scores(a, b):
        return lax.dot_general(a, b, (((1,), (1,)), ((), ())), preferred_element_type=jnp.float32)

    def times(a, b):
        return jnp.dot(a, b, preferred_element_type=jnp.float32)

    def turned_times(a, b):
        return lax.dot_general(a, b, (((0,), (0,)), ((), ())), preferred_element_type=jnp.float32)

    def text_half(k, d, diagonal=False):
        at = pl.ds(pl.multiple_of(k * half, half), half)
        t, i = txt[at, :], img[d]
        w = weights(scores(t, i), col_c[at, :], row_f[d, 0:1, :])
        if diagonal:
            t_id = lax.broadcasted_iota(jnp.int32, w.shape, 0) + k * half
            i_id = lax.broadcasted_iota(jnp.int32, w.shape, 1)
            w = w - jnp.where(t_id == i_id, 2.0, 0.0)
        w = w.astype(jnp.bfloat16)
        acc_t[at, :] += times(w, i)
        acc_i[d] += turned_times(w, t)

    def image_half(d, k, g):
        at = pl.ds(pl.multiple_of(k * half, half), half)
        t_at = pl.ds(pl.multiple_of(g * rows, rows), rows)
        t, i = txt[t_at, :], img[d, at, :]
        w = weights(scores(i, t), row_c[d, at, :], col_f[g, 0:1, :]).astype(jnp.bfloat16)
        acc_i[d, at, :] += times(w, t)
        acc_t[t_at, :] += turned_times(w, i)

    def loop(count, body):
        def step(k, carry):
            body(k)
            return carry

        lax.fori_loop(0, count, step, 0)

    load_t.wait()
    load_i.wait()
    loop(2, lambda k: text_half(k, 0, True))

    @pl.when(core == 0)
    def _():
        def take(j):
            send_2(j).wait_recv()
            pass_1(j).start()

        @pl.when(first)
        def _():
            pl.semaphore_wait(ready_sem.at[2], len(mid))
            for j in range(PIECES):
                send_routes(j, [route for route in ROUTES_2 if route[:2] in mid])

        f_1.wait_recv()
        for j in range(PIECES):
            send_1(j).wait_recv()
        loop(2, lambda k: text_half(k, 1))

        @pl.when(first)
        def _():
            pl.semaphore_wait(ready_sem.at[0], len(later) + 1)
            f_2.start()
            for j in range(PIECES):
                send_routes(j, [route for route in ROUTES_2 if route[:2] in later])

        def start_t():
            pl.semaphore_wait(go_sem, 1)
            for j in range(PIECES):
                send_t(j).start()

        pl.when(last)(start_t)
        take(0)
        f_2.wait_recv()
        f_1_pass.start()
        row_c[2] = upright(row_f[2, 0:1, :])

        def both(k):
            @pl.when(k == 0)
            def _():
                take(1)

            @pl.when(k == 1)
            def _():
                pass_2()
                pl.when(jnp.logical_not(last))(start_t)
                take(2)
                take(3)

            image_half(2, k, 0)

        loop(2, both)
        f_t.wait_recv()
        col_c[pl.ds(rows, rows), :] = upright(col_f[1, 0:1, :])
        send_t(0).wait_recv()
        send_t(1).wait_recv()
        loop(3, lambda d: text_half(2, d))
        out_t[pl.ds(0, half), :] = acc_t[pl.ds(rows, half), :].astype(jnp.bfloat16)
        send_t(2).wait_recv()
        send_t(3).wait_recv()
        back_t(0).start()
        back_t(1).start()

        def ending(k):
            text_half(3, 2 - k)

            @pl.when(k == 0)
            def _():
                def on(j):
                    back_1(j).wait_recv()
                    both = acc_i[2, piece(j), :] + in_1[piece(j), :].astype(jnp.float32)
                    out_2[piece(j), :] = both.astype(jnp.bfloat16)
                    start_back(j)

                for j in range(PIECES):
                    on(j)

            @pl.when(k == 1)
            def _():
                out_1[...] = acc_i[1].astype(jnp.bfloat16)
                loop(PIECES, lambda j: back_1(j).start())

        loop(3, ending)
        out_t[pl.ds(half, half), :] = acc_t[pl.ds(rows + half, half), :].astype(jnp.bfloat16)
        back_t(2).start()
        back_t(3).start()

    @pl.when(core == 1)
    def _():
        f_t.wait_recv()
        col_c[pl.ds(rows, rows), :] = upright(col_f[1, 0:1, :])
        send_t(0).wait_recv()
        send_t(1).wait_recv()
        pl.semaphore_signal(go_sem, inc=1, device_id=sibling, device_id_type=MESH)

        @pl.when(last)
        def _():
            for j in range(PIECES):
                send_2(j).start()

        text_half(2, 0)
        f_1.wait_recv()
        row_c[1] = upright(row_f[1, 0:1, :])

        def near(k):
            send_1(2 * k).wait_recv()
            send_1(2 * k + 1).wait_recv()

            @pl.when(k == 0)
            def _():
                @pl.when(first)
                def _():
                    pl.semaphore_wait(ready_sem.at[2], len(mid))
                    pl.semaphore_wait(ready_sem.at[0], len(later) + 1)
                    f_2.start()

                @pl.when(jnp.logical_not(last))
                def _():
                    for j in range(PIECES):
                        start_2(j)

            image_half(1, k, 0)

        loop(2, near)
        send_t(2).wait_recv()
        send_t(3).wait_recv()

        def beside(k):
            text_half(2 + jnp.minimum(k, 1), 1 - k // 2)

            @pl.when(k == 1)
            def _():
                out_1[...] = acc_i[1].astype(jnp.bfloat16)
                loop(PIECES, lambda j: back_1(j).start())
                pass_2()

        loop(3, beside)
        f_2.wait_recv()
        row_c[2] = upright(row_f[2, 0:1, :])

        def far(k):
            send_2(2 * k).wait_recv()
            send_2(2 * k + 1).wait_recv()

            def side(g):
                image_half(2, k, 1 - g)

                @pl.when(jnp.logical_and(k == 1, g == 0))
                def _():
                    out_t[...] = acc_t[pl.ds(rows, rows), :].astype(jnp.bfloat16)
                    loop(PIECES, lambda j: back_t(j).start())

            loop(2, side)
            at = pl.ds(pl.multiple_of(k * half, half), half)
            out_2[at, :] = acc_i[2, at, :].astype(jnp.bfloat16)
            for j in range(2):

                @pl.when(k == j)
                def _():
                    start_back(2 * j)
                    start_back(2 * j + 1)

        loop(2, far)

        def near_back(j):
            back_1(j).wait_recv()
            acc_i[0, piece(j), :] += in_1[piece(j), :].astype(jnp.float32)

        loop(PIECES, near_back)

    pass_back()

    def finish(j):
        back_t(j).wait_recv()
        grad_txt[piece(j), :] = acc_t[piece(j), :] + in_t[piece(j), :].astype(jnp.float32)
        back_2(j).wait_recv()
        grad_img[piece(j), :] = acc_i[0, piece(j), :] + in_2[piece(j), :].astype(jnp.float32)

    loop(PIECES, finish)

    f_t.wait_send()
    f_2.wait_send()
    f_1.wait_send()

    def sent(j):
        for copy in (send_t, send_2, send_1, back_t, back_1, back_2):
            copy(j).wait_send()

    loop(PIECES, sent)

    pass_2(done=True)
    pass_back(done=True)


def store(grad_img, grad_txt, img_out, txt_out, sem):
    rows = grad_img.shape[0] // PIECES
    copies = []
    for j in range(PIECES):
        for k, (src, dst) in enumerate(((grad_img, img_out), (grad_txt, txt_out))):
            at = pl.ds(j * rows, rows)
            copies.append(pltpu.make_async_copy(src.at[at], dst.at[at], sem.at[k, j]))
    for copy in copies:
        copy.start()
    for copy in copies:
        copy.wait()


def local(n_blk, images, texts, row_lse, col_lse):
    rows, width = images.shape
    scale = 2.0 / math.sqrt(width)
    bf16, f32 = jnp.bfloat16, jnp.float32
    any_spec = pl.BlockSpec(memory_space=pl.ANY)
    hbm_spec = pl.BlockSpec(memory_space=pltpu.HBM)
    vmem_spec = pl.BlockSpec(memory_space=pltpu.VMEM)
    grads = pl.pallas_call(
        functools.partial(kernel, n_blk, scale),
        out_shape=[pltpu.VMEM((rows, width), f32)] * 2,
        in_specs=[hbm_spec] * 4,
        out_specs=[vmem_spec] * 2,
        scratch_shapes=[
            pltpu.VMEM((2 * rows, width), bf16),
            pltpu.VMEM((3, rows, width), bf16),
            pltpu.VMEM((3, 8, rows), f32),
            pltpu.VMEM((2, 8, rows), f32),
            pltpu.VMEM((3, rows, 128), f32),
            pltpu.VMEM((2 * rows, 128), f32),
            pltpu.VMEM((2 * rows, width), f32),
            pltpu.VMEM((3, rows, width), f32),
        ]
        + [pltpu.VMEM((rows, width), bf16)] * 6
        + [
            pltpu.VMEM((rows,), bf16),
            pltpu.VMEM((rows,), bf16),
            pltpu.SemaphoreType.DMA((4,)),
            pltpu.SemaphoreType.DMA((6, PIECES)),
            pltpu.SemaphoreType.DMA((6, PIECES)),
            pltpu.SemaphoreType.DMA((3,)),
            pltpu.SemaphoreType.DMA((3,)),
            pltpu.SemaphoreType.REGULAR,
            pltpu.SemaphoreType.REGULAR((3,)),
            pltpu.VMEM((2, RELAY_ROWS, width), bf16),
            pltpu.SemaphoreType.DMA((2,)),
            pltpu.SemaphoreType.DMA((2,)),
        ],
        compiler_params=pltpu.CompilerParams(
            collective_id=0, has_side_effects=True, vmem_limit_bytes=48 * 2**20
        ),
        cost_estimate=pl.CostEstimate(
            flops=18 * 2 * rows * rows * width,
            bytes_accessed=12 * rows * width,
            transcendentals=6 * rows * rows,
        ),
        name="contrastive",
    )(
        pltpu.with_memory_space_constraint(texts, pltpu.HBM),
        pltpu.with_memory_space_constraint(images, pltpu.HBM),
        pltpu.with_memory_space_constraint(row_lse, pltpu.HBM),
        pltpu.with_memory_space_constraint(col_lse, pltpu.HBM),
    )
    return tuple(
        pl.pallas_call(
            store,
            out_shape=[jax.ShapeDtypeStruct((rows, width), f32)] * 2,
            in_specs=[vmem_spec] * 2,
            out_specs=[any_spec] * 2,
            scratch_shapes=[pltpu.SemaphoreType.DMA((2, PIECES))],
            compiler_params=pltpu.CompilerParams(vmem_limit_bytes=16 * 2**20),
            name="store",
        )(*grads)
    )


def solution(mesh):
    both = ("blk", "grp")
    return jax.shard_map(
        functools.partial(local, mesh.shape["blk"]),
        mesh=mesh,
        in_specs=(P(both, None), P(both, None), P(both), P(both)),
        out_specs=(P(both, None), P(both, None)),
        check_vma=False,
    )
```

```python
import functools
import math

import jax
import jax.numpy as jnp
from jax import lax
from jax.experimental import pallas as pl
from jax.experimental.pallas import tpu as pltpu
from jax.sharding import PartitionSpec as P

MESH = pl.DeviceIdType.MESH
LSE_TOP = 10.0
LOG2E = math.log2(math.e)
PIECES = 4
NX, NZ = 4, 8
ROUTES_2 = (
    (2, 0, 0, 64),
    (2, 1, 64, 64),
    (1, 0, 128, 64),
    (1, 1, 192, 64),
    (2, 2, 256, 64),
    (2, 3, 320, 64),
    (0, 7, 384, 64),
    (2, 4, 448, 64),
)
ROUTES_BACK = (
    (3, 0, 0, 64),
    (1, 6, 64, 64),
    (1, 7, 128, 32),
    (2, 6, 160, 32),
    (1, 5, 192, 64),
    (0, 0, 256, 64),
    (1, 4, 320, 64),
    (2, 0, 384, 64),
    (1, 3, 448, 64),
)
RELAY_ROWS = 64
Z_SOON, Z_MID = 1, 3


def kernel(
    n_blk,
    scale,
    texts_in,
    images_in,
    row_lse,
    col_lse,
    grad_img,
    grad_txt,
    txt,
    img,
    row_f,
    col_f,
    row_c,
    col_c,
    acc_t,
    acc_i,
    out_t,
    out_1,
    out_2,
    in_t,
    in_1,
    in_2,
    lse_0,
    lse_1,
    load_sem,
    send_sem,
    recv_sem,
    f_send,
    f_recv,
    go_sem,
    ready_sem,
    relay,
    relay_send,
    relay_recv,
):
    rows = texts_in.shape[0]
    half = rows // 2
    part = rows // PIECES
    c = lax.axis_index("blk")
    h = lax.axis_index("grp")
    core = lax.rem(c, 2)
    other = (c, 1 - h)
    sibling = (c + 1 - 2 * core, h)
    ahead = (lax.rem(c + 2, n_blk), h)
    behind = (lax.rem(c + n_blk - 2, n_blk), h)

    x, z, y = lax.rem(c // 2, NX), lax.rem(c // (2 * NX), NZ), c // (2 * NX * NZ)

    def chip(cx, cz, cy):
        return ((cy * NZ + cz) * NX + cx) * 2 + core, h

    def is_at(cx, cz):
        return jnp.logical_and(x == cx, z == cz)

    first, last = is_at(0, 0), is_at(NX - 1, NZ - 1)

    def piece(j, base=0):
        return pl.ds(pl.multiple_of(base + j * part, part), part)

    def remote(src, dst, sends, recvs, to):
        return pltpu.make_async_remote_copy(
            src_ref=src, dst_ref=dst, send_sem=sends, recv_sem=recvs, device_id=to, device_id_type=MESH
        )

    def remote_k(kind, j, src, dst, to):
        return remote(src, dst, send_sem.at[kind, j], recv_sem.at[kind, j], to)

    def send_t(j):
        return remote_k(0, j, texts_in.at[piece(j)], txt.at[piece(j, rows)], other)

    def send_2(j):
        return remote_k(1, j, images_in.at[piece(j)], img.at[2, piece(j)], behind)

    def send_1(j):
        return remote_k(2, j, images_in.at[piece(j)], img.at[1, piece(j)], sibling)

    def pass_1(j):
        return remote_k(2, j, img.at[2, piece(j)], img.at[1, piece(j)], sibling)

    def back_t(j):
        return remote_k(3, j, out_t.at[piece(j)], in_t.at[piece(j)], other)

    def back_1(j):
        return remote_k(4, j, out_1.at[piece(j)], in_1.at[piece(j)], sibling)

    def back_2(j):
        return remote_k(5, j, out_2.at[piece(j)], in_2.at[piece(j)], ahead)

    def send_on(routes, final, src, dst, kind, slot, j):
        for cx, cz, r, n in routes:
            if r // part != j:
                continue
            sem = send_sem.at[kind, j]
            if (cx, cz) == final:
                copy = remote(src.at[pl.ds(r, n)], dst.at[pl.ds(r, n)], sem, recv_sem.at[kind, j], chip(cx, cz, 1 - y))
            else:
                there = relay.at[slot, pl.ds(0, n)]
                copy = remote(src.at[pl.ds(r, n)], there, sem, relay_recv.at[slot], chip(cx, cz, 1 - y))
            copy.start()

    FIRST, LAST = (0, 0), (NX - 1, NZ - 1)

    def send_routes(j, routes=ROUTES_2):
        send_on(routes, LAST, images_in, img.at[2], 1, 0, j)

    def start_2(j):
        @pl.when(jnp.logical_not(first))
        def _():
            send_2(j).start()

        @pl.when(first)
        def _():
            send_routes(j)

    def start_back(j):
        @pl.when(jnp.logical_not(last))
        def _():
            back_2(j).start()

        @pl.when(last)
        def _():
            send_on(ROUTES_BACK, FIRST, out_2, in_2, 5, 1, j)

    def on_route(routes, final, slot, kind, dst, done):
        for cx, cz, r, n in routes:
            if (cx, cz) == final:
                continue

            @pl.when(is_at(cx, cz))
            def _():
                here = relay.at[slot, pl.ds(0, n)]
                if not done:
                    if slot == 0:
                        pl.semaphore_wait(ready_sem.at[1], 1)
                    remote(here, here, relay_send.at[slot], relay_recv.at[slot], chip(*final, y)).wait_recv()
                copy = remote(here, dst.at[pl.ds(r, n)], relay_send.at[slot], recv_sem.at[kind, r // part], chip(*final, y))
                if done:
                    copy.wait_send()
                else:
                    copy.start()

    def pass_2(done=False):
        on_route(ROUTES_2, LAST, 0, 1, img.at[2], done)

    def pass_back(done=False):
        on_route(ROUTES_BACK, FIRST, 1, 5, in_2, done)

    f_t = remote(col_f.at[0], col_f.at[1], f_send.at[0], f_recv.at[0], other)
    f_2 = remote(row_f.at[0], row_f.at[2], f_send.at[1], f_recv.at[1], behind)
    f_1 = remote(row_f.at[0], row_f.at[1], f_send.at[2], f_recv.at[2], sibling)
    f_1_pass = remote(row_f.at[2], row_f.at[1], f_send.at[2], f_recv.at[2], sibling)

    load_t = pltpu.make_async_copy(texts_in, txt.at[pl.ds(0, rows)], load_sem.at[0])
    load_i = pltpu.make_async_copy(images_in, img.at[0], load_sem.at[1])

    lse = (lse_0, lse_1)
    load_l = [
        pltpu.make_async_copy(row_lse, lse_0, load_sem.at[2]),
        pltpu.make_async_copy(col_lse, lse_1, load_sem.at[3]),
    ]
    for copy in load_l:
        copy.start()

    barrier = pltpu.get_barrier_semaphore()

    def greet(device):
        pl.semaphore_signal(barrier, inc=1, device_id=device, device_id_type=MESH)

    def tell(role, device):
        pl.semaphore_signal(ready_sem.at[role], inc=1, device_id=device, device_id_type=MESH)

    between = [(cx, cz) for cx, cz, _, _ in ROUTES_2 if (cx, cz) != LAST]
    soon = [at for at in between if at[1] <= Z_SOON]
    mid = [at for at in between if Z_SOON < at[1] <= Z_MID]
    later = [at for at in between if at[1] > Z_MID]
    back = [(cx, cz) for cx, cz, _, _ in ROUTES_BACK if (cx, cz) != FIRST]

    for device in (other, sibling, behind):
        greet(device)

    @pl.when(jnp.logical_not(last))
    def _():
        greet(ahead)

    greetings = 4 + jnp.where(first, len(soon) - 1, 0) + jnp.where(last, len(between) + len(back), 0)
    for at in between:

        @pl.when(is_at(*at))
        def _():
            greet(chip(*LAST, y))

    for at in soon:

        @pl.when(is_at(*at))
        def _():
            greet(chip(*FIRST, 1 - y))

    for at in mid + later:
        greetings += jnp.where(is_at(*at), 1, 0)

    for at in back:
        greetings += jnp.where(is_at(*at), 1, 0)

        @pl.when(is_at(*at))
        def _():
            greet(chip(*LAST, 1 - y))

    @pl.when(first)
    def _():
        for at in mid + later:
            greet(chip(*at, 1 - y))
        for at in back:
            greet(chip(*at, y))

    load_t.start()
    load_i.start()
    for k, line in enumerate((row_f, col_f)):
        load_l[k].wait()
        factor = jnp.exp(LSE_TOP - lse[k][...].astype(jnp.float32))
        line[0] = jnp.broadcast_to(factor.reshape(1, rows), (8, rows))
    pl.semaphore_wait(barrier, greetings)

    @pl.when(last)
    def _():
        tell(0, chip(*FIRST, 1 - y))
        for at in between:
            tell(1, chip(*at, y))

    for at in mid + later:

        @pl.when(is_at(*at))
        def _():
            tell(2 if at in mid else 0, chip(*FIRST, 1 - y))

    f_t.start()

    @pl.when(jnp.logical_not(first))
    def _():
        f_2.start()


    @pl.when(core == 0)
    def _():
        @pl.when(jnp.logical_not(first))
        def _():
            for j in range(PIECES):
                send_2(j).start()

        @pl.when(first)
        def _():
            for j in range(PIECES):
                send_routes(j, [route for route in ROUTES_2 if route[:2] in soon])

    @pl.when(core == 1)
    def _():
        f_1.start()
        for j in range(PIECES):
            send_t(j).start()
        for j in range(PIECES):
            send_1(j).start()

    acc_t[...] = jnp.zeros(acc_t.shape, jnp.float32)
    acc_i[...] = jnp.zeros(acc_i.shape, jnp.float32)

    def upright(line):
        return jnp.broadcast_to(line, (128, rows)).T

    col_c[pl.ds(0, rows), :] = upright(col_f[0, 0:1, :])

    def weights(s, upright_f, line_f):
        wide = jnp.concatenate([upright_f] * (s.shape[1] // 128), axis=1)
        return jnp.exp2(s * (scale * LOG2E) - LSE_TOP * LOG2E) * (wide + line_f)

    def scores(a, b):
        return lax.dot_general(a, b, (((1,), (1,)), ((), ())), preferred_element_type=jnp.float32)

    def times(a, b):
        return jnp.dot(a, b, preferred_element_type=jnp.float32)

    def turned_times(a, b):
        return lax.dot_general(a, b, (((0,), (0,)), ((), ())), preferred_element_type=jnp.float32)

    def text_half(k, d, diagonal=False):
        at = pl.ds(pl.multiple_of(k * half, half), half)
        t, i = txt[at, :], img[d]
        w = weights(scores(t, i), col_c[at, :], row_f[d, 0:1, :])
        if diagonal:
            t_id = lax.broadcasted_iota(jnp.int32, w.shape, 0) + k * half
            i_id = lax.broadcasted_iota(jnp.int32, w.shape, 1)
            w = w - jnp.where(t_id == i_id, 2.0, 0.0)
        w = w.astype(jnp.bfloat16)
        acc_t[at, :] += times(w, i)
        acc_i[d] += turned_times(w, t)

    def image_half(d, k, g):
        at = pl.ds(pl.multiple_of(k * half, half), half)
        t_at = pl.ds(pl.multiple_of(g * rows, rows), rows)
        t, i = txt[t_at, :], img[d, at, :]
        w = weights(scores(i, t), row_c[d, at, :], col_f[g, 0:1, :]).astype(jnp.bfloat16)
        acc_i[d, at, :] += times(w, t)
        acc_t[t_at, :] += turned_times(w, i)

    def loop(count, body):
        def step(k, carry):
            body(k)
            return carry

        lax.fori_loop(0, count, step, 0)

    load_t.wait()
    load_i.wait()
    loop(2, lambda k: text_half(k, 0, True))

    @pl.when(core == 0)
    def _():
        def take(j):
            send_2(j).wait_recv()
            pass_1(j).start()

        @pl.when(first)
        def _():
            pl.semaphore_wait(ready_sem.at[2], len(mid))
            for j in range(PIECES):
                send_routes(j, [route for route in ROUTES_2 if route[:2] in mid])

        f_1.wait_recv()
        for j in range(PIECES):
            send_1(j).wait_recv()
        loop(2, lambda k: text_half(k, 1))

        @pl.when(first)
        def _():
            pl.semaphore_wait(ready_sem.at[0], len(later) + 1)
            f_2.start()
            for j in range(PIECES):
                send_routes(j, [route for route in ROUTES_2 if route[:2] in later])

        def start_t():
            pl.semaphore_wait(go_sem, 1)
            for j in range(PIECES):
                send_t(j).start()

        pl.when(last)(start_t)
        take(0)
        f_2.wait_recv()
        f_1_pass.start()
        row_c[2] = upright(row_f[2, 0:1, :])

        def both(k):
            @pl.when(k == 0)
            def _():
                take(1)

            @pl.when(k == 1)
            def _():
                pass_2()
                pl.when(jnp.logical_not(last))(start_t)
                take(2)
                take(3)

            image_half(2, k, 0)

        loop(2, both)
        f_t.wait_recv()
        col_c[pl.ds(rows, rows), :] = upright(col_f[1, 0:1, :])
        send_t(0).wait_recv()
        send_t(1).wait_recv()
        loop(3, lambda d: text_half(2, d))
        out_t[pl.ds(0, half), :] = acc_t[pl.ds(rows, half), :].astype(jnp.bfloat16)
        back_t(0).start()
        back_t(1).start()
        send_t(2).wait_recv()
        send_t(3).wait_recv()

        def ending(k):
            text_half(3, 2 - k)

            @pl.when(k == 0)
            def _():
                def on(j):
                    back_1(j).wait_recv()
                    both = acc_i[2, piece(j), :] + in_1[piece(j), :].astype(jnp.float32)
                    out_2[piece(j), :] = both.astype(jnp.bfloat16)
                    start_back(j)

                for j in range(PIECES):
                    on(j)

            @pl.when(k == 1)
            def _():
                out_1[...] = acc_i[1].astype(jnp.bfloat16)
                loop(PIECES, lambda j: back_1(j).start())

        loop(3, ending)
        out_t[pl.ds(half, half), :] = acc_t[pl.ds(rows + half, half), :].astype(jnp.bfloat16)
        back_t(2).start()
        back_t(3).start()

    @pl.when(core == 1)
    def _():
        f_t.wait_recv()
        col_c[pl.ds(rows, rows), :] = upright(col_f[1, 0:1, :])
        send_t(0).wait_recv()
        send_t(1).wait_recv()
        pl.semaphore_signal(go_sem, inc=1, device_id=sibling, device_id_type=MESH)

        @pl.when(last)
        def _():
            for j in range(PIECES):
                send_2(j).start()

        text_half(2, 0)
        f_1.wait_recv()
        row_c[1] = upright(row_f[1, 0:1, :])

        def near(k):
            send_1(2 * k).wait_recv()
            send_1(2 * k + 1).wait_recv()

            @pl.when(k == 0)
            def _():
                @pl.when(first)
                def _():
                    pl.semaphore_wait(ready_sem.at[2], len(mid))
                    pl.semaphore_wait(ready_sem.at[0], len(later) + 1)
                    f_2.start()

                @pl.when(jnp.logical_not(last))
                def _():
                    for j in range(PIECES):
                        start_2(j)

            image_half(1, k, 0)

        loop(2, near)
        send_t(2).wait_recv()
        send_t(3).wait_recv()

        def beside(k):
            text_half(2 + jnp.minimum(k, 1), 1 - k // 2)

            @pl.when(k == 1)
            def _():
                out_1[...] = acc_i[1].astype(jnp.bfloat16)
                loop(PIECES, lambda j: back_1(j).start())
                pass_2()

        loop(3, beside)
        f_2.wait_recv()
        row_c[2] = upright(row_f[2, 0:1, :])

        def far(k):
            send_2(2 * k).wait_recv()
            send_2(2 * k + 1).wait_recv()

            def side(g):
                image_half(2, k, 1 - g)

                @pl.when(jnp.logical_and(k == 1, g == 0))
                def _():
                    out_t[...] = acc_t[pl.ds(rows, rows), :].astype(jnp.bfloat16)
                    loop(PIECES, lambda j: back_t(j).start())

            loop(2, side)
            at = pl.ds(pl.multiple_of(k * half, half), half)
            out_2[at, :] = acc_i[2, at, :].astype(jnp.bfloat16)
            for j in range(2):

                @pl.when(k == j)
                def _():
                    start_back(2 * j)
                    start_back(2 * j + 1)

        loop(2, far)

        def near_back(j):
            back_1(j).wait_recv()
            acc_i[0, piece(j), :] += in_1[piece(j), :].astype(jnp.float32)

        loop(PIECES, near_back)

    pass_back()

    def finish(j):
        back_t(j).wait_recv()
        grad_txt[piece(j), :] = acc_t[piece(j), :] + in_t[piece(j), :].astype(jnp.float32)
        back_2(j).wait_recv()
        grad_img[piece(j), :] = acc_i[0, piece(j), :] + in_2[piece(j), :].astype(jnp.float32)

    loop(PIECES, finish)

    f_t.wait_send()
    f_2.wait_send()
    f_1.wait_send()

    def sent(j):
        for copy in (send_t, send_2, send_1, back_t, back_1, back_2):
            copy(j).wait_send()

    loop(PIECES, sent)

    pass_2(done=True)
    pass_back(done=True)


def store(grad_img, grad_txt, img_out, txt_out, sem):
    rows = grad_img.shape[0] // PIECES
    copies = []
    for j in range(PIECES):
        for k, (src, dst) in enumerate(((grad_img, img_out), (grad_txt, txt_out))):
            at = pl.ds(j * rows, rows)
            copies.append(pltpu.make_async_copy(src.at[at], dst.at[at], sem.at[k, j]))
    for copy in copies:
        copy.start()
    for copy in copies:
        copy.wait()


def local(n_blk, images, texts, row_lse, col_lse):
    rows, width = images.shape
    scale = 2.0 / math.sqrt(width)
    bf16, f32 = jnp.bfloat16, jnp.float32
    any_spec = pl.BlockSpec(memory_space=pl.ANY)
    hbm_spec = pl.BlockSpec(memory_space=pltpu.HBM)
    vmem_spec = pl.BlockSpec(memory_space=pltpu.VMEM)
    grads = pl.pallas_call(
        functools.partial(kernel, n_blk, scale),
        out_shape=[pltpu.VMEM((rows, width), f32)] * 2,
        in_specs=[hbm_spec] * 4,
        out_specs=[vmem_spec] * 2,
        scratch_shapes=[
            pltpu.VMEM((2 * rows, width), bf16),
            pltpu.VMEM((3, rows, width), bf16),
            pltpu.VMEM((3, 8, rows), f32),
            pltpu.VMEM((2, 8, rows), f32),
            pltpu.VMEM((3, rows, 128), f32),
            pltpu.VMEM((2 * rows, 128), f32),
            pltpu.VMEM((2 * rows, width), f32),
            pltpu.VMEM((3, rows, width), f32),
        ]
        + [pltpu.VMEM((rows, width), bf16)] * 6
        + [
            pltpu.VMEM((rows,), bf16),
            pltpu.VMEM((rows,), bf16),
            pltpu.SemaphoreType.DMA((4,)),
            pltpu.SemaphoreType.DMA((6, PIECES)),
            pltpu.SemaphoreType.DMA((6, PIECES)),
            pltpu.SemaphoreType.DMA((3,)),
            pltpu.SemaphoreType.DMA((3,)),
            pltpu.SemaphoreType.REGULAR,
            pltpu.SemaphoreType.REGULAR((3,)),
            pltpu.VMEM((2, RELAY_ROWS, width), bf16),
            pltpu.SemaphoreType.DMA((2,)),
            pltpu.SemaphoreType.DMA((2,)),
        ],
        compiler_params=pltpu.CompilerParams(
            collective_id=0, has_side_effects=True, vmem_limit_bytes=48 * 2**20
        ),
        cost_estimate=pl.CostEstimate(
            flops=18 * 2 * rows * rows * width,
            bytes_accessed=12 * rows * width,
            transcendentals=6 * rows * rows,
        ),
        name="contrastive",
    )(
        pltpu.with_memory_space_constraint(texts, pltpu.HBM),
        pltpu.with_memory_space_constraint(images, pltpu.HBM),
        pltpu.with_memory_space_constraint(row_lse, pltpu.HBM),
        pltpu.with_memory_space_constraint(col_lse, pltpu.HBM),
    )
    return tuple(
        pl.pallas_call(
            store,
            out_shape=[jax.ShapeDtypeStruct((rows, width), f32)] * 2,
            in_specs=[vmem_spec] * 2,
            out_specs=[any_spec] * 2,
            scratch_shapes=[pltpu.SemaphoreType.DMA((2, PIECES))],
            compiler_params=pltpu.CompilerParams(vmem_limit_bytes=16 * 2**20),
            name="store",
        )(*grads)
    )


def solution(mesh):
    both = ("blk", "grp")
    return jax.shard_map(
        functools.partial(local, mesh.shape["blk"]),
        mesh=mesh,
        in_specs=(P(both, None), P(both, None), P(both), P(both)),
        out_specs=(P(both, None), P(both, None)),
        check_vma=False,
    )
```
